256 devices in a mesh: band: 8 (over x, z_hi), grid: 32 (over z_lo, y, core).
Axes of the slice: x: 4, y: 4, z: 8 (z_hi: 2, z_lo: 4; z = z_hi * 4 + z_lo), core: 2. Of those that a mesh axis runs over, the one named last changes fastest.
Arguments:
- orbitals: float32 [64, 128, 16384], P('band', 'grid'), may hold values from -6 to 6
- plan: int32 [2, 8, 2], replicated, may hold values from 0 to 1
Outputs:
- exchange: float32 [64, 128, 16384], P('band', 'grid')
The draws below stay inside these ranges and needn't reach their ends.
All inputs are finite; a program needn't handle non-finite values.
Results may differ from the reference program's by a relative error of at most 0.0003.
Values sent between devices are 32-bit elements; how exact they have to be, the bound alone decides.
No kernel may reach another device: no remote copies, remote signals or barrier semaphores. Data moves between devices by JAX's collectives and lax.ppermute only.
A program may use at most 128 MiB of HBM per device.

```python
import math
import jax
import jax.numpy as jnp

GRID = 128
SUB = 4
NSUB = 2
ROUNDS = 2
N_BAND = 8


def draw_orbitals(key, part):
    key = jax.random.fold_in(key, 11)
    shape = (N_BAND * NSUB * SUB, GRID, GRID * GRID)
    values = jax.random.normal(key, shape, jnp.float32)
    return jnp.clip(values, -6.0, 6.0)


def set_ends(drawn, rng, least, high):
    longest = drawn.shape.index(max(drawn.shape))
    spots = []
    for shift in (0, 1):
        where = [jax.random.randint(jax.random.fold_in(rng, axis), (), 0, length) for axis, length in enumerate(drawn.shape)]
        where[longest] = (where[longest] + shift) % drawn.shape[longest]
        spots.append(tuple(where))
    return drawn.at[spots[0]].set(least).at[spots[1]].set(high)


def setup_inputs(seed: int = 0) -> dict:
    key_list = jax.random.split(jax.random.key(seed), 3)
    return {
        "orbitals": draw_orbitals(jax.random.fold_in(key_list[2], 71), 0),
        "plan": set_ends(jax.random.randint(key_list[1], (ROUNDS, N_BAND, 2), 0, NSUB), jax.random.fold_in(key_list[1], 1), 0, NSUB - 1).astype(jnp.int32),
    }


def screened_kernel(n):
    full = jnp.arange(n, dtype=jnp.float32)
    half = jnp.arange(n // 2 + 1, dtype=jnp.float32)
    lam_full = 2.0 - 2.0 * jnp.cos(full * (2.0 * math.pi / n))
    lam_half = 2.0 - 2.0 * jnp.cos(half * (2.0 * math.pi / n))
    screen = (4.0 * math.pi / n) ** 2
    kern = 1.0 / (screen + lam_full[:, None, None] + lam_full[None, :, None] + lam_half[None, None, :])
    anchor = (full[:, None, None] == 0) & (full[None, :, None] == 0) & (half[None, None, :] == 0)
    return jnp.where(anchor, jnp.zeros_like(kern), kern)


def reference(orbitals, plan):
    blocks = orbitals.reshape(N_BAND, NSUB, SUB, GRID, GRID, GRID)
    kern = screened_kernel(GRID)

    def poisson(density):
        spectrum = jnp.fft.rfftn(density)
        return jnp.fft.irfftn(spectrum * kern, s=density.shape).astype(orbitals.dtype)

    total = jnp.zeros_like(blocks)
    for step in range(ROUNDS):
        shift_by = step + 1
        for block in range(N_BAND):
            partner_block = (block - shift_by) % N_BAND
            first = plan[step, block, 0]
            second = plan[step, block, 1]
            own = blocks[block][first]
            partner = blocks[partner_block][second]
            density = own[:, None] * partner[None, :]
            potential = jax.vmap(jax.vmap(poisson))(density)
            own_terms = -jnp.sum(potential * partner[None, :], axis=1)
            partner_terms = -jnp.sum(potential * own[:, None], axis=0)
            total = total.at[block, first].add(own_terms)
            total = total.at[partner_block, second].add(partner_terms)
    return total.reshape(N_BAND * NSUB * SUB, GRID, GRID * GRID)
```

```python
import functools
import math

import jax
import jax.numpy as jnp
import ml_dtypes
import numpy as np
from jax import lax
from jax.experimental import pallas as pl
from jax.experimental.pallas import tpu as pltpu
from jax.sharding import PartitionSpec as P

GRID = 128
SUB = 4
NSUB = 2
ROUNDS = 2
CORES = 2
YS = 4
ZS = 4
PLANES = 4
ROWS = GRID * PLANES
HALF = SUB // CORES
QUARTER = GRID // YS
CHUNKS = ((0, (0,)), (1, (0, 1)), (0, (1,)))
F32 = jnp.float32
BF16 = jnp.bfloat16


@functools.cache
def tables():
    index = np.arange(GRID, dtype=np.int64)
    angle = (index[:, None] * index[None, :] % GRID) * (2.0 * math.pi / GRID)
    cas = (np.cos(angle) + np.sin(angle)).astype(np.float32)
    high = cas.astype(ml_dtypes.bfloat16)
    low = (cas - high.astype(np.float32)).astype(ml_dtypes.bfloat16)
    zero = np.zeros_like(high)
    right = np.block([[high, low], [high, zero]])
    left = np.block([[high, high], [low, zero]])
    roots = 2.0 - 2.0 * np.cos(index * (2.0 * math.pi / GRID))
    screen = (4.0 * math.pi / GRID) ** 2
    shift = screen + roots[:, None] + roots[None, :]
    spread = np.sqrt(shift + shift * shift / 4.0)
    decay = 1.0 / (1.0 + shift / 2.0 + spread)
    scale = 1.0 / (2.0 * spread * GRID**2)
    mean = np.zeros((1, GRID))
    mean[0, 0] = 2.0 * spread[0, 0] / (GRID * screen)
    chips = np.stack([decay ** (8 * k) for k in range(YS)])
    runs = np.stack([decay**32, decay**64, 1.0 / (1.0 - decay**GRID)])
    as32 = lambda value: np.asarray(value, dtype=np.float32)
    return right, left, as32(decay), as32(scale), as32(mean), as32(chips), as32(runs)


def split(value):
    high = value.astype(BF16)
    low = (value - high.astype(F32)).astype(BF16)
    return high, low


def times_right(value, table):
    full = jnp.dot(jnp.concatenate(split(value), axis=1), table, preferred_element_type=F32)
    return full[:, :GRID] + full[:, GRID:]


def times_left(value, table):
    full = jnp.dot(table, jnp.concatenate(split(value), axis=0), preferred_element_type=F32)
    return full[:GRID] + full[GRID:]


def place():
    spot = lax.axis_index("grid")
    return spot // (YS * CORES), (spot // CORES) % YS, spot % CORES


def quarter_of(which):
    return pl.ds(pl.multiple_of(which * QUARTER, QUARTER), QUARTER)


def pick_kernel(plan, orbitals, index, *rest):
    outs, sems = rest[:-1], rest[-1]
    band_count = lax.axis_size("band")
    band_me = lax.axis_index("band")
    core = place()[2]
    copies = []
    for step in range(ROUNDS):
        later = plan[step, (band_me + step + 1) % band_count, 1] * SUB
        index[step] = plan[step, band_me, 0] * SUB
        index[ROUNDS + step] = later
        for cross in range(2):
            target = core if cross == 0 else 1 - core
            for j in range(HALF):
                number = len(copies)
                copy = pltpu.make_async_copy(
                    orbitals.at[pl.ds(later + target * HALF + j, 1)], outs[number], sems.at[number]
                )
                copy.start()
                copies.append(copy)
    for copy in copies:
        copy.wait()


def pick(plan, orbitals):
    count = ROUNDS * 2 * HALF
    hbm = pl.BlockSpec(memory_space=pl.ANY)
    smem = pl.BlockSpec(memory_space=pltpu.SMEM)
    outs = pl.pallas_call(
        pick_kernel,
        in_specs=[smem, hbm],
        out_specs=[smem] + [hbm] * count,
        out_shape=[jax.ShapeDtypeStruct((2 * ROUNDS,), jnp.int32)]
        + [jax.ShapeDtypeStruct((1, ROWS, GRID), F32)] * count,
        scratch_shapes=[pltpu.SemaphoreType.DMA((count,))],
        compiler_params=pltpu.CompilerParams(vmem_limit_bytes=2 << 20),
        name="pick",
    )(plan, orbitals)
    index, blocks = outs[0], outs[1:]
    sends = {}
    for step in range(ROUNDS):
        for cross in range(2):
            for j in range(HALF):
                sends[step, cross, j] = blocks[(step * 2 + cross) * HALF + j]
    return index, sends


def forward_kernel(pairs, index, own_a, own_b, part_a, part_b, right, left, decay, scale, spec, *rest):
    outs, lines = rest[:YS], rest[YS]
    _, y, core = place()
    pair = pl.program_id(0) * SUB + pl.program_id(1)
    for source, (own, part) in enumerate(((own_a, part_a), (own_b, part_b))):
        lines[...] = times_right(own[0] * part[0], right[...])
        half = (core if source == 0 else 1 - core) * PLANES
        for x in range(0, PLANES, 2):
            two = jnp.concatenate(
                [lines[pl.ds(x + k, GRID, stride=PLANES), :] for k in range(2)], axis=1
            )
            two = times_left(two, left[...])
            for k in range(2):
                spec[0, half + x + k] = two[:, k * GRID : (k + 1) * GRID] * scale[...]
    total = spec[0, 0, 0:1, :]
    for x in range(1, 2 * PLANES):
        total = total + spec[0, x, 0:1, :]
    base = pl.multiple_of(pair * (2 * QUARTER), 2 * QUARTER)
    for d in range(YS):
        rows = quarter_of((y + d) % YS)
        ratio = decay[rows, :]
        planes = [spec[0, x, rows, :] for x in range(2 * PLANES)]
        ahead, behind = planes[0], planes[-1]
        for x in range(1, 2 * PLANES):
            ahead = planes[x] + ratio * ahead
            behind = planes[-1 - x] + ratio * behind
        outs[d][pl.ds(base, QUARTER), :] = ahead
        outs[d][pl.ds(base + QUARTER, QUARTER), :] = behind

        @pl.when(pair == 0)
        def _():
            outs[d][pl.ds(pairs * 2 * QUARTER, 8), :] = jnp.zeros((8, GRID), F32)

        outs[d][pl.ds(pairs * 2 * QUARTER + pair, 1), :] = total


def own_spec(step):
    return pl.BlockSpec((1, ROWS, GRID), lambda j, i, index: (index[step] + i, 0, 0))


def whole(shape):
    return pl.BlockSpec(shape, lambda *_: (0,) * len(shape))


def forward(step, count, index, own, part):
    right, left, decay, scale = tables()[:4]
    pairs = count * SUB
    message = (pairs * 2 * QUARTER + 8, GRID)
    band = pl.BlockSpec((1, ROWS, GRID), lambda j, i, index: (j, 0, 0))
    outs = pl.pallas_call(
        functools.partial(forward_kernel, pairs),
        grid_spec=pltpu.PrefetchScalarGridSpec(
            num_scalar_prefetch=1,
            grid=(count, SUB),
            in_specs=[own_spec(step)] * 2
            + [band] * 2
            + [whole((2 * GRID, 2 * GRID))] * 2
            + [whole((GRID, GRID))] * 2,
            out_specs=[
                pl.BlockSpec((1, 2 * PLANES, GRID, GRID), lambda j, i, index: (j * SUB + i, 0, 0, 0))
            ]
            + [whole(message)] * YS,
            scratch_shapes=[pltpu.VMEM((ROWS, GRID), F32)],
        ),
        out_shape=[jax.ShapeDtypeStruct((pairs, 2 * PLANES, GRID, GRID), F32)]
        + [jax.ShapeDtypeStruct(message, F32)] * YS,
        compiler_params=pltpu.CompilerParams(vmem_limit_bytes=16 << 20),
        cost_estimate=pl.CostEstimate(
            flops=pairs * 2048 * 2 * 65536, bytes_accessed=pairs << 20, transcendentals=0
        ),
        name="forward",
    )(index, own[0], own[1], part[0], part[1], right, left, decay, scale)
    return outs[0], outs[1:]


def run_kernel(pairs, a, b, c, d, chips, out):
    _, y, _ = place()
    rows = quarter_of(y)
    got = (a, b, c, d)
    from_chip = [(y - k + YS) % YS for k in range(YS)]
    ahead = [chips[YS - 1 - chip, rows, :] for chip in from_chip]
    behind = [chips[chip, rows, :] for chip in from_chip]
    for pair in range(pairs):
        base = pair * 2 * QUARTER
        for weights, start in ((ahead, base), (behind, base + QUARTER)):
            at = slice(start, start + QUARTER)
            out[at, :] = sum(got[k][at, :] * weights[k] for k in range(YS))
    at = slice(pairs * 2 * QUARTER, pairs * 2 * QUARTER + 8)
    out[at, :] = sum(got[k][at, :] for k in range(YS))


def two_kernel(pairs, mine, other, runs, out):
    z, y, _ = place()
    power = runs[0, quarter_of(y), :]
    odd = (jnp.zeros(power.shape, jnp.int32) + z % 2) == 1
    ones = jnp.ones_like(power)
    first = jnp.where(odd, ones, power)
    second = jnp.where(odd, power, ones)
    for pair in range(pairs):
        base = pair * 2 * QUARTER
        at = slice(base, base + QUARTER)
        out[at, :] = mine[at, :] * first + other[at, :] * second
        at = slice(base + QUARTER, base + 2 * QUARTER)
        out[at, :] = mine[at, :] * second + other[at, :] * first
    at = slice(pairs * 2 * QUARTER, pairs * 2 * QUARTER + 8)
    out[at, :] = mine[at, :] + other[at, :]


def edges_kernel(pairs, a, b, c, d, near, mine, other, chips, runs, *rest):
    outs, held = rest[:YS], rest[YS]
    z, y, _ = place()
    rows = quarter_of(y)
    got = (a, b, c, d)
    step, run, two, wrap = chips[1, rows, :], runs[0, rows, :], runs[1, rows, :], runs[2, rows, :]
    odd = (jnp.zeros(step.shape, jnp.int32) + z % 2) == 1
    for k in range(YS):
        held[(y - k + YS) % YS] = got[k][...]
    for pair in range(pairs):
        base = pair * 2 * QUARTER
        ahead = slice(base, base + QUARTER)
        behind = slice(base + QUARTER, base + 2 * QUARTER)
        from_left = (other[ahead, :] + two * mine[ahead, :]) * wrap
        from_right = (other[behind, :] + two * mine[behind, :]) * wrap
        from_left = jnp.where(odd, near[ahead, :] + run * from_left, from_left)
        from_right = jnp.where(odd, from_right, near[behind, :] + run * from_right)
        for chip in range(YS):
            chip_ahead = held[chip, ahead, :]
            held[chip, ahead, :] = from_left
            from_left = chip_ahead + step * from_left
        for chip in reversed(range(YS)):
            chip_behind = held[chip, behind, :]
            held[chip, behind, :] = from_right
            from_right = chip_behind + step * from_right
    at = slice(pairs * 2 * QUARTER, pairs * 2 * QUARTER + 8)
    total = mine[at, :] + other[at, :]
    for k in range(YS):
        outs[k][...] = held[(y - k + YS) % YS]
        outs[k][at, :] = total


def small_call(kernel, pairs, args, count, name, scratch=()):
    shape = args[0].shape
    outs = pl.pallas_call(
        functools.partial(kernel, pairs),
        in_specs=[pl.BlockSpec(memory_space=pltpu.VMEM)] * len(args),
        out_specs=[pl.BlockSpec(memory_space=pltpu.VMEM)] * count,
        out_shape=[jax.ShapeDtypeStruct(shape, F32)] * count,
        scratch_shapes=scratch,
        compiler_params=pltpu.CompilerParams(vmem_limit_bytes=8 << 20),
        cost_estimate=pl.CostEstimate(
            flops=8 * args[0].size, bytes_accessed=4 * args[0].size * (len(args) + count), transcendentals=0
        ),
        name=name,
    )(*args)
    return outs


def backward_kernel(
    pairs, index, spec, a, b, c, d, own_a, own_b, part_a, part_b, right, left, decay, mean,
    part_out_a, part_out_b, own_out_a, own_out_b, field, lines
):
    edges = (a, b, c, d)
    _, y, core = place()
    j, i = pl.program_id(0), pl.program_id(1)
    pair = j * SUB + i
    base = pl.multiple_of(pair * (2 * QUARTER), 2 * QUARTER)
    for k in range(YS):
        rows = quarter_of((y + k) % YS)
        ratio = decay[rows, :]
        planes = [spec[0, x, rows, :] for x in range(2 * PLANES)]
        ahead = edges[k][pl.ds(base, QUARTER), :]
        behind = edges[k][pl.ds(base + QUARTER, QUARTER), :]
        sums = []
        for x in range(2 * PLANES):
            ahead = planes[x] + ratio * ahead
            sums.append(ahead)
        for x in reversed(range(2 * PLANES)):
            behind = ratio * behind
            field[x, rows, :] = sums[x] + behind
            behind = planes[x] + behind
    average = a[pl.ds(pairs * 2 * QUARTER + pair, 1), :] * mean[...]
    for x in range(2 * PLANES):
        field[x, 0:1, :] = field[x, 0:1, :] - average
    for source, (own, part, part_out, own_out) in enumerate(
        ((own_a, part_a, part_out_a, own_out_a), (own_b, part_b, part_out_b, own_out_b))
    ):
        half = (core if source == 0 else 1 - core) * PLANES
        for x in range(0, PLANES, 2):
            two = jnp.concatenate([field[half + x + k] for k in range(2)], axis=1)
            two = times_left(two, left[...])
            for k in range(2):
                lines[pl.ds(x + k, GRID, stride=PLANES), :] = two[:, k * GRID : (k + 1) * GRID]
        potential = times_right(lines[...], right[...])
        to_part = potential * own[0]
        to_own = potential * part[0]

        @pl.when(i == 0)
        def _():
            part_out[0] = -to_part

        @pl.when(i != 0)
        def _():
            part_out[0] = part_out[0] - to_part

        @pl.when(j == 0)
        def _():
            own_out[i] = -to_own

        @pl.when(j != 0)
        def _():
            own_out[i] = own_out[i] - to_own


def backward(step, count, index, spec, edges, own, part):
    right, left, decay, _, mean = tables()[:5]
    pairs = count * SUB
    message = edges[0].shape
    band = pl.BlockSpec((1, ROWS, GRID), lambda j, i, index: (j, 0, 0))
    outs = pl.pallas_call(
        functools.partial(backward_kernel, pairs),
        grid_spec=pltpu.PrefetchScalarGridSpec(
            num_scalar_prefetch=1,
            grid=(count, SUB),
            in_specs=[
                pl.BlockSpec((1, 2 * PLANES, GRID, GRID), lambda j, i, index: (j * SUB + i, 0, 0, 0))
            ]
            + [whole(message)] * YS
            + [own_spec(step)] * 2
            + [band] * 2
            + [whole((2 * GRID, 2 * GRID))] * 2
            + [whole((GRID, GRID)), whole((1, GRID))],
            out_specs=[band] * 2 + [whole((SUB, ROWS, GRID))] * 2,
            scratch_shapes=[pltpu.VMEM((2 * PLANES, GRID, GRID), F32), pltpu.VMEM((ROWS, GRID), F32)],
        ),
        out_shape=[jax.ShapeDtypeStruct((count, ROWS, GRID), F32)] * 2
        + [jax.ShapeDtypeStruct((SUB, ROWS, GRID), F32)] * 2,
        compiler_params=pltpu.CompilerParams(vmem_limit_bytes=20 << 20),
        cost_estimate=pl.CostEstimate(
            flops=pairs * 2048 * 2 * 65536, bytes_accessed=pairs << 20, transcendentals=0
        ),
        name="backward",
    )(index, spec, *edges, own[0], own[1], part[0], part[1], right, left, decay, mean)
    return outs


def total_kernel(kinds, index, *refs):
    terms, out = refs[:-1], refs[-1]
    core = place()[2]
    i = pl.program_id(0)
    sums = [jnp.zeros((ROWS, GRID), F32) for _ in range(NSUB)]
    for (slot, cross, j), ref in zip(kinds, terms):
        base = index[slot]
        for sub in range(NSUB):
            use = base == sub * SUB
            if cross is not None:
                target = core if cross == 0 else 1 - core
                use = use & (i == target * HALF + j)
            sums[sub] = sums[sub] + jnp.where(use, ref[0], 0.0)
    for sub in range(NSUB):
        out[sub, 0] = sums[sub]


def add_up(index, own_terms, part_terms):
    kinds, args, specs = [], [], []
    for step, value in own_terms:
        kinds.append((step, None, None))
        args.append(value)
        specs.append(pl.BlockSpec((1, ROWS, GRID), lambda i, index: (i, 0, 0)))
    for step, cross, j, at, value in part_terms:
        kinds.append((ROUNDS + step, cross, j))
        args.append(value)
        specs.append(pl.BlockSpec((1, ROWS, GRID), lambda i, index, at=at: (at, 0, 0)))
    return pl.pallas_call(
        functools.partial(total_kernel, tuple(kinds)),
        grid_spec=pltpu.PrefetchScalarGridSpec(
            num_scalar_prefetch=1,
            grid=(SUB,),
            in_specs=specs,
            out_specs=pl.BlockSpec((NSUB, 1, ROWS, GRID), lambda i, index: (0, i, 0, 0)),
        ),
        out_shape=jax.ShapeDtypeStruct((NSUB, SUB, ROWS, GRID), F32),
        compiler_params=pltpu.CompilerParams(vmem_limit_bytes=24 << 20),
        name="add_up",
    )(index, *args)


def body(orbitals, plan):
    bands = lax.axis_size("band")
    spots = lax.axis_size("grid")

    def move(value, target):
        pairs = []
        for band in range(bands):
            for spot in range(spots):
                z, y, core = spot // (YS * CORES), (spot // CORES) % YS, spot % CORES
                b2, z2, y2, c2 = target(band, z, y, core)
                pairs.append((band * spots + spot, (b2 % bands) * spots + (z2 * YS + y2 % YS) * CORES + c2))
        return lax.ppermute(value, ("band", "grid"), pairs)

    def swap_cores(value):
        return move(value, lambda b, z, y, c: (b, z, y, 1 - c))

    chips, runs = tables()[5:7]
    blocks = orbitals.reshape(NSUB * SUB, PLANES, GRID, GRID).transpose(0, 2, 1, 3)
    blocks = blocks.reshape(NSUB * SUB, ROWS, GRID)
    index, sends = pick(plan, blocks)
    own = (blocks, swap_cores(blocks))
    got = {}
    for step, members in CHUNKS:
        for j in members:
            for cross in range(2):
                got[step, cross, j] = move(
                    sends[step, cross, j],
                    lambda b, z, y, c, s=step + 1, f=cross: (b + s, z, y, 1 - c if f else c),
                )
    own_terms, part_terms = [], []
    for step, members in CHUNKS:
        count = len(members)
        pairs = count * SUB
        part = [
            jnp.concatenate([got[step, cross, j] for j in members], axis=0) if count > 1 else got[step, cross, members[0]]
            for cross in range(2)
        ]
        spec, sums = forward(step, count, index, own, part)
        sums = [sums[0]] + [
            move(sums[d], lambda b, z, y, c, d=d: (b, z, y + d, c)) for d in range(1, YS)
        ]
        run = small_call(run_kernel, pairs, [*sums, chips], 1, "run")[0]
        near = move(run, lambda b, z, y, c: (b, z ^ 1, y, c))
        two = small_call(two_kernel, pairs, [run, near, runs], 1, "two")[0]
        far = move(two, lambda b, z, y, c: (b, z ^ 2, y, c))
        edges = small_call(
            edges_kernel, pairs, [*sums, near, two, far, chips, runs], YS, "edges",
            [pltpu.VMEM((YS, *run.shape), F32)],
        )
        edges = [edges[0]] + [
            move(edges[d], lambda b, z, y, c, d=d: (b, z, y + YS - d, c)) for d in range(1, YS)
        ]
        part_same, part_cross, own_same, own_cross = backward(step, count, index, spec, edges, own, part)
        for cross, value in ((0, part_same), (1, part_cross)):
            value = move(value, lambda b, z, y, c, s=step + 1, f=cross: (b - s, z, y, 1 - c if f else c))
            for at, j in enumerate(members):
                part_terms.append((step, cross, j, at, value))
        own_terms.append((step, own_same))
        own_terms.append((step, swap_cores(own_cross)))
    total = add_up(index, own_terms, part_terms)
    total = total.reshape(NSUB * SUB, GRID, PLANES, GRID).transpose(0, 2, 1, 3)
    return total.reshape(NSUB * SUB, PLANES, GRID * GRID)


def solution(mesh):
    in_specs = (P("band", "grid", None), P())
    out_specs = P("band", "grid", None)
    return jax.shard_map(body, mesh=mesh, in_specs=in_specs, out_specs=out_specs, check_vma=False)
```

```python
import functools
import math

import jax
import jax.numpy as jnp
import ml_dtypes
import numpy as np
from jax import lax
from jax.experimental import pallas as pl
from jax.experimental.pallas import tpu as pltpu
from jax.sharding import PartitionSpec as P

GRID = 128
SUB = 4
NSUB = 2
ROUNDS = 2
CORES = 2
YS = 4
ZS = 4
PLANES = 4
ROWS = GRID * PLANES
HALF = SUB // CORES
QUARTER = GRID // YS
EDGE = 2 * QUARTER
CHAINS = ((1, (0, 1)), (0, (0, 1)))
F32 = jnp.float32
BF16 = jnp.bfloat16


@functools.cache
def tables():
    index = np.arange(GRID, dtype=np.int64)
    angle = (index[:, None] * index[None, :] % GRID) * (2.0 * math.pi / GRID)
    cas = (np.cos(angle) + np.sin(angle)).astype(np.float32)
    high = cas.astype(ml_dtypes.bfloat16)
    low = (cas - high.astype(np.float32)).astype(ml_dtypes.bfloat16)
    zero = np.zeros_like(high)
    right = np.block([[high, low], [high, zero]])
    left = np.block([[high, high], [low, zero]])
    roots = 2.0 - 2.0 * np.cos(index * (2.0 * math.pi / GRID))
    screen = (4.0 * math.pi / GRID) ** 2
    shift = screen + roots[:, None] + roots[None, :]
    spread = np.sqrt(shift + shift * shift / 4.0)
    decay = 1.0 / (1.0 + shift / 2.0 + spread)
    scale = 1.0 / (2.0 * spread * GRID**2)
    mean = np.zeros((1, GRID))
    mean[0, 0] = 2.0 * spread[0, 0] / (GRID * screen)
    chips = np.stack([decay ** (8 * k) for k in range(YS)])
    runs = np.stack([decay**32, decay**64, 1.0 / (1.0 - decay**GRID)])
    as32 = lambda value: np.asarray(value, dtype=np.float32)
    return right, left, as32(decay), as32(scale), as32(mean), as32(chips), as32(runs)


def split(value):
    high = value.astype(BF16)
    low = (value - high.astype(F32)).astype(BF16)
    return high, low


def times_right(value, table):
    full = jnp.dot(jnp.concatenate(split(value), axis=1), table, preferred_element_type=F32)
    return full[:, :GRID] + full[:, GRID:]


def times_left(value, table):
    full = jnp.dot(table, jnp.concatenate(split(value), axis=0), preferred_element_type=F32)
    return full[:GRID] + full[GRID:]


def place():
    spot = lax.axis_index("grid")
    return spot // (YS * CORES), (spot // CORES) % YS, spot % CORES


def quarter_of(which):
    return pl.ds(pl.multiple_of(which * QUARTER, QUARTER), QUARTER)


def array(shape, dtype=F32):
    return jax.ShapeDtypeStruct(tuple(shape), dtype)


HBM = pl.BlockSpec(memory_space=pltpu.HBM)
VMEM = pl.BlockSpec(memory_space=pltpu.VMEM)
SMEM = pl.BlockSpec(memory_space=pltpu.SMEM)


def launch(kernel, token, args, in_specs, out_specs, out_shape, name, limit, grid=(), scratch=(), after=()):
    ins, outs, waits = len(args), len(out_shape), 1 + len(after)
    unread = pl.BlockSpec(memory_space=pl.ANY)

    def ordered(*refs):
        kernel(*refs[:ins], *refs[ins + waits : ins + waits + outs], *refs[ins + waits + outs + 1 :])

    result = pl.pallas_call(
        ordered,
        grid=grid,
        in_specs=[*in_specs, *[unread] * waits],
        out_specs=[*out_specs, unread],
        scratch_shapes=list(scratch),
        out_shape=[*out_shape, array(token.shape)],
        compiler_params=pltpu.CompilerParams(vmem_limit_bytes=limit << 20),
        cost_estimate=pl.CostEstimate(flops=0, bytes_accessed=0, transcendentals=0),
        name=name,
    )(*args, token, *after)
    return result[:-1], result[-1]


def message(pairs):
    return array((pairs * EDGE + 8, GRID))


def pairs_of(ref):
    return ref.shape[0] // EDGE


def copy_all(copies, sems):
    started = []
    for number, (source, target) in enumerate(copies):
        copy = pltpu.make_async_copy(source, target, sems.at[number])
        copy.start()
        started.append(copy)
    for copy in started:
        copy.wait()


def pick_kernel(plan, own_a, own_b, index, first, second, sems):
    band_count = lax.axis_size("band")
    band_me = lax.axis_index("band")
    core = place()[2]
    index[0] = plan[0, band_me, 0]
    index[1] = plan[1, (band_me + 2) % band_count, 1]
    index[2] = plan[0, (band_me + 1) % band_count, 1]
    index[3] = plan[1, band_me, 0]
    copies = []
    for step, out in enumerate((first, second)):
        start = index[ROUNDS + step] * SUB + core * HALF
        for source, own in enumerate((own_a, own_b)):
            copies.append((own.at[pl.ds(start, HALF)], out.at[source]))
    copy_all(copies, sems)


def pick(token, plan, own):
    two = array((CORES, HALF, ROWS, GRID))
    outs, token = launch(
        pick_kernel, token, [plan, *own], [SMEM, HBM, VMEM], [SMEM] + [VMEM] * 2,
        [array((2 * ROUNDS,), jnp.int32), two, two], "pick", 2,
        scratch=[pltpu.SemaphoreType.DMA((2 * CORES,))],
    )
    return *outs, token


def pick_own_kernel(index, own_a, own_b, out, sems):
    copy_all(
        [
            (own.at[pl.ds(index[step] * SUB, SUB)], out.at[step, source])
            for step in range(ROUNDS)
            for source, own in enumerate((own_a, own_b))
        ],
        sems,
    )


def pick_own(token, index, own):
    (out,), token = launch(
        pick_own_kernel, token, [index, *own], [SMEM, HBM, VMEM], [VMEM],
        [array((ROUNDS, CORES, SUB, ROWS, GRID))], "pick_own", 2,
        scratch=[pltpu.SemaphoreType.DMA((ROUNDS * CORES,))],
    )
    return out, token


def forward_kernel(step, member, own, part, right, left, decay, scale, spec, a, b, c, d, lines):
    outs = (a, b, c, d)
    _, y, core = place()
    j = pl.program_id(0)
    for i in range(SUB):
        for source in range(CORES):
            spot = i * CORES + source
            lines[spot] = times_right(own[step, source, i] * part[source, member + j], right[...])
            half = (core if source == 0 else 1 - core) * PLANES
            for x in range(0, PLANES, 2):
                two = jnp.concatenate(
                    [lines[spot, pl.ds(x + k, GRID, stride=PLANES), :] for k in range(2)], axis=1
                )
                two = times_left(two, left[...])
                for k in range(2):
                    spec[j * SUB + i, half + x + k] = two[:, k * GRID : (k + 1) * GRID] * scale[...]
    for i in range(SUB):
        pair = j * SUB + i
        base = pl.multiple_of(pair * EDGE, EDGE)
        total = spec[pair, 0, 0:1, :]
        for x in range(1, 2 * PLANES):
            total = total + spec[pair, x, 0:1, :]
        for k in range(YS):
            rows = quarter_of((y + k) % YS)
            ratio = decay[rows, :]
            planes = [spec[pair, x, rows, :] for x in range(2 * PLANES)]
            ahead, behind = planes[0], planes[-1]
            for x in range(1, 2 * PLANES):
                ahead = planes[x] + ratio * ahead
                behind = planes[-1 - x] + ratio * behind
            outs[k][pl.ds(base, QUARTER), :] = ahead
            outs[k][pl.ds(base + QUARTER, QUARTER), :] = behind
            outs[k][pl.ds(pairs_of(a) * EDGE + pair, 1), :] = total


def forward(token, step, members, own, part):
    right, left, decay, scale = tables()[:4]
    pairs = len(members) * SUB
    outs, token = launch(
        functools.partial(forward_kernel, step, members[0]),
        token,
        [own, part, right, left, decay, scale],
        [VMEM] * 6,
        [VMEM] * (1 + YS),
        [array((pairs, 2 * PLANES, GRID, GRID))] + [message(pairs)] * YS,
        "forward", 12, grid=(len(members),),
        scratch=[pltpu.VMEM((SUB * CORES, ROWS, GRID), F32)],
    )
    return outs[0], outs[1:], token


def run_kernel(a, b, c, d, chips, out):
    _, y, _ = place()
    rows = quarter_of(y)
    got = (a, b, c, d)
    from_chip = [(y - k + YS) % YS for k in range(YS)]
    ahead = [chips[YS - 1 - chip, rows, :] for chip in from_chip]
    behind = [chips[chip, rows, :] for chip in from_chip]
    for pair in range(pairs_of(out)):
        base = pair * EDGE
        for weights, start in ((ahead, base), (behind, base + QUARTER)):
            at = slice(start, start + QUARTER)
            out[at, :] = sum(got[k][at, :] * weights[k] for k in range(YS))
    at = slice(pairs_of(out) * EDGE, pairs_of(out) * EDGE + 8)
    out[at, :] = sum(got[k][at, :] for k in range(YS))


def two_kernel(mine, other, runs, out):
    z, y, _ = place()
    power = runs[0, quarter_of(y), :]
    odd = (jnp.zeros(power.shape, jnp.int32) + z % 2) == 1
    ones = jnp.ones_like(power)
    first = jnp.where(odd, ones, power)
    second = jnp.where(odd, power, ones)
    for pair in range(pairs_of(out)):
        base = pair * EDGE
        at = slice(base, base + QUARTER)
        out[at, :] = mine[at, :] * first + other[at, :] * second
        at = slice(base + QUARTER, base + 2 * QUARTER)
        out[at, :] = mine[at, :] * second + other[at, :] * first
    at = slice(pairs_of(mine) * EDGE, pairs_of(mine) * EDGE + 8)
    out[at, :] = mine[at, :] + other[at, :]


def edges_kernel(a, b, c, d, near, mine, other, chips, runs, *rest):
    outs, held = rest[:YS], rest[YS]
    z, y, _ = place()
    rows = quarter_of(y)
    got = (a, b, c, d)
    step, run, two, wrap = chips[1, rows, :], runs[0, rows, :], runs[1, rows, :], runs[2, rows, :]
    odd = (jnp.zeros(step.shape, jnp.int32) + z % 2) == 1
    for k in range(YS):
        held[(y - k + YS) % YS] = got[k][...]
    for pair in range(pairs_of(a)):
        base = pair * EDGE
        ahead = slice(base, base + QUARTER)
        behind = slice(base + QUARTER, base + 2 * QUARTER)
        from_left = (other[ahead, :] + two * mine[ahead, :]) * wrap
        from_right = (other[behind, :] + two * mine[behind, :]) * wrap
        from_left = jnp.where(odd, near[ahead, :] + run * from_left, from_left)
        from_right = jnp.where(odd, from_right, near[behind, :] + run * from_right)
        for chip in range(YS):
            chip_ahead = held[chip, ahead, :]
            held[chip, ahead, :] = from_left
            from_left = chip_ahead + step * from_left
        for chip in reversed(range(YS)):
            chip_behind = held[chip, behind, :]
            held[chip, behind, :] = from_right
            from_right = chip_behind + step * from_right
    at = slice(pairs_of(mine) * EDGE, pairs_of(mine) * EDGE + 8)
    total = mine[at, :] + other[at, :]
    for k in range(YS):
        outs[k][...] = held[(y - k + YS) % YS]
        outs[k][at, :] = total


def small(kernel, token, args, count, name, scratch=(), after=()):
    return launch(
        kernel, token, args, [VMEM] * len(args), [VMEM] * count, [array(args[0].shape)] * count, name, 6,
        scratch=scratch, after=after,
    )


def backward_kernel(step, member, prior, extra, spec, a, b, c, d, own, part, right, left, decay, mean, *rest):
    before, (part_out, own_out_a, own_out_b, field, lines) = rest[: prior + extra], rest[prior + extra :]
    j = pl.program_id(0)
    edges = (a, b, c, d)
    _, y, core = place()
    for i in range(SUB):
        pair = j * SUB + i
        base = pl.multiple_of(pair * EDGE, EDGE)
        for k in range(YS):
            rows = quarter_of((y + k) % YS)
            ratio = decay[rows, :]
            planes = [spec[pair, x, rows, :] for x in range(2 * PLANES)]
            ahead = edges[k][pl.ds(base, QUARTER), :]
            behind = edges[k][pl.ds(base + QUARTER, QUARTER), :]
            sums = []
            for x in range(2 * PLANES):
                ahead = planes[x] + ratio * ahead
                sums.append(ahead)
            for x in reversed(range(2 * PLANES)):
                behind = ratio * behind
                field[i, x, rows, :] = sums[x] + behind
                behind = planes[x] + behind
        average = a[pl.ds(pairs_of(a) * EDGE + pair, 1), :] * mean[...]
        for x in range(2 * PLANES):
            field[i, x, 0:1, :] = field[i, x, 0:1, :] - average
    for source, own_out in enumerate((own_out_a, own_out_b)):
        half = (core if source == 0 else 1 - core) * PLANES
        added = None
        for i in range(SUB):
            spot = i * CORES + source
            for x in range(0, PLANES, 2):
                two = jnp.concatenate([field[i, half + x + k] for k in range(2)], axis=1)
                two = times_left(two, left[...])
                for k in range(2):
                    lines[spot, pl.ds(x + k, GRID, stride=PLANES), :] = two[:, k * GRID : (k + 1) * GRID]
            potential = times_right(lines[spot], right[...])
            to_part = potential * own[step, source, i]
            to_own = potential * part[source, member + j]
            added = to_part if added is None else added + to_part
            if prior:
                own_out[0, i] = before[source][0, i] - to_own
            else:
                own_out[0, i] = jnp.where(j == 0, 0.0, own_out[0, i]) - to_own
        part_out[source, j] = -added
    if extra:
        own_out_b[1] = before[prior][0]


def backward(token, step, members, spec, edges, own, part, prior=(), extra=()):
    right, left, decay, _, mean = tables()[:5]
    args = [spec, *edges, own, part, right, left, decay, mean, *prior, *extra]
    outs, token = launch(
        functools.partial(backward_kernel, step, members[0], len(prior), len(extra)),
        token,
        args,
        [VMEM] * len(args),
        [VMEM] * 3,
        [
            array((CORES, len(members), ROWS, GRID)),
            array((1, SUB, ROWS, GRID)),
            array((1 + len(extra), SUB, ROWS, GRID)),
        ],
        "backward", 12, grid=(len(members),),
        scratch=[
            pltpu.VMEM((SUB, 2 * PLANES, GRID, GRID), F32),
            pltpu.VMEM((SUB * CORES, ROWS, GRID), F32),
        ],
    )
    return outs[0], outs[1:], token


def early_kernel(index, own_first, own_second, swapped, same, cross, out):
    core = place()[2]
    for i in range(SUB):
        out[index[0] * SUB + i] = own_first[0, i] + swapped[0, i]
        out[(NSUB - 1 - index[0]) * SUB + i] = jnp.zeros((ROWS, GRID), F32)
    for i in range(SUB):
        band = index[1] * SUB + i
        out[band] = out[band] + (own_second[0, i] + swapped[1, i])
    for part, target in ((same, core), (cross, 1 - core)):
        for member in range(HALF):
            band = index[ROUNDS + 1] * SUB + target * HALF + member
            out[band] = out[band] + part[0, member]


def add_early(token, index, terms):
    (total,), token = launch(
        early_kernel, token, [index, *terms], [SMEM] + [VMEM] * len(terms),
        [VMEM], [array((NSUB * SUB, ROWS, GRID))], "add_early", 4,
    )
    return total, token


def late_kernel(index, total, same, cross, out, fresh, sems):
    core = place()[2]
    base = index[ROUNDS] * SUB
    other = (NSUB - 1) * SUB - base
    rest = pltpu.make_async_copy(total.at[pl.ds(other, SUB)], out.at[pl.ds(other, SUB)], sems.at[0])
    rest.start()
    for k, (part, target) in enumerate(((same, core), (cross, 1 - core))):
        for member in range(HALF):
            at = target * HALF + member
            fresh[at] = total[base + at] + part[0, member]
    added = pltpu.make_async_copy(fresh, out.at[pl.ds(base, SUB)], sems.at[1])
    added.start()
    rest.wait()
    added.wait()


def add_late(token, index, total, terms):
    (total,), token = launch(
        late_kernel, token, [index, total, *terms], [SMEM] + [VMEM] * 3, [HBM],
        [array(total.shape)], "add_late", 4,
        scratch=[pltpu.VMEM((SUB, ROWS, GRID), F32), pltpu.SemaphoreType.DMA((2,))],
    )
    return total


def body(orbitals, plan):
    bands = lax.axis_size("band")
    spots = lax.axis_size("grid")

    def move(value, target):
        pairs = []
        for band in range(bands):
            for spot in range(spots):
                z, y, core = spot // (YS * CORES), (spot // CORES) % YS, spot % CORES
                b2, z2, y2, c2 = target(band, z, y, core)
                pairs.append((band * spots + spot, (b2 % bands) * spots + (z2 * YS + y2 % YS) * CORES + c2))
        return lax.ppermute(value, ("band", "grid"), pairs)

    def swap_cores(value):
        return move(value, lambda b, z, y, c: (b, z, y, 1 - c))

    def shift(value, steps):
        return move(value, lambda b, z, y, c: (b + steps, z, y, c))

    def along_y(messages, sign):
        return [messages[0]] + [
            move(messages[k], lambda b, z, y, c, k=k: (b, z, y + YS + sign * k, c)) for k in range(1, YS)
        ]

    chips, runs = tables()[5:7]
    blocks = orbitals.reshape(NSUB * SUB, PLANES, GRID, GRID).transpose(0, 2, 1, 3)
    blocks = blocks.reshape(NSUB * SUB, ROWS, GRID)
    both = (blocks, swap_cores(blocks))
    token = jnp.zeros((8, GRID), F32)
    index, *sends, token = pick(token, plan, both)
    parts = [shift(sends[0], 1), shift(sends[1], -2)]
    own, token = pick_own(token, index, both)
    chains = [{} for _ in CHAINS]

    def start(at):
        nonlocal token
        step, members = CHAINS[at]
        chain = chains[at]
        chain["spec"], sums, token = forward(token, step, members, own, parts[step])
        chain["sums"] = along_y(sums, 1)

    def run(at):
        nonlocal token
        chain = chains[at]
        (chain["run"],), token = small(run_kernel, token, [*chain["sums"], chips], 1, "run")
        chain["near"] = move(chain["run"], lambda b, z, y, c: (b, z ^ 1, y, c))

    def two(at):
        nonlocal token
        chain = chains[at]
        (chain["two"],), token = small(two_kernel, token, [chain["run"], chain["near"], runs], 1, "two")
        chain["far"] = move(chain["two"], lambda b, z, y, c: (b, z ^ 2, y, c))

    def edges(at, after=()):
        nonlocal token
        chain = chains[at]
        args = [*chain["sums"], chain["near"], chain["two"], chain["far"], chips, runs]
        outs, token = small(
            edges_kernel, token, args, YS, "edges", [pltpu.VMEM((YS, *chain["run"].shape), F32)], after
        )
        chain["edges"] = along_y(outs, -1)

    def finish(at, prior=(), extra=()):
        nonlocal token
        step, members = CHAINS[at]
        chain = chains[at]
        terms, sums, token = backward(
            token, step, members, chain["spec"], chain["edges"], own, parts[step], prior, extra
        )
        return terms, sums

    def give_back(at, terms):
        steps = (-1, 2)[CHAINS[at][0]]
        return [shift(terms[:1], steps), move(terms[1:], lambda b, z, y, c: (b + steps, z, y, 1 - c))]

    second, first = range(len(CHAINS))
    start(second)
    run(second)
    start(first)
    two(second)
    run(first)
    edges(second)
    two(first)
    terms_b, sums_b = finish(second)
    edges(first)
    terms_a, sums_a = finish(first, extra=sums_b[1:])
    total, token = add_early(
        token, index, [sums_a[0], sums_b[0], swap_cores(sums_a[1]), *give_back(second, terms_b)]
    )
    final = give_back(first, terms_a)
    total = add_late(token, index, total, final)
    total = total.reshape(NSUB * SUB, GRID, PLANES, GRID).transpose(0, 2, 1, 3)
    return total.reshape(NSUB * SUB, PLANES, GRID * GRID)


def solution(mesh):
    in_specs = (P("band", "grid", None), P())
    out_specs = P("band", "grid", None)
    return jax.shard_map(body, mesh=mesh, in_specs=in_specs, out_specs=out_specs, check_vma=False)
```

```python
import functools
import math

import jax
import jax.numpy as jnp
import ml_dtypes
import numpy as np
from jax import lax
from jax.experimental import pallas as pl
from jax.experimental.pallas import tpu as pltpu
from jax.sharding import PartitionSpec as P

GRID = 128
SUB = 4
NSUB = 2
ROUNDS = 2
CORES = 2
YS = 4
ZS = 4
PLANES = 4
ROWS = GRID * PLANES
HALF = SUB // CORES
QUARTER = GRID // YS
EDGE = 2 * QUARTER
CHAINS = ((1, (0, 1)), (0, (0,)), (0, (1,)))
F32 = jnp.float32
BF16 = jnp.bfloat16


@functools.cache
def tables():
    index = np.arange(GRID, dtype=np.int64)
    angle = (index[:, None] * index[None, :] % GRID) * (2.0 * math.pi / GRID)
    cas = (np.cos(angle) + np.sin(angle)).astype(np.float32)
    high = cas.astype(ml_dtypes.bfloat16)
    low = (cas - high.astype(np.float32)).astype(ml_dtypes.bfloat16)
    zero = np.zeros_like(high)
    right = np.block([[high, low], [high, zero]])
    left = np.block([[high, high], [low, zero]])
    roots = 2.0 - 2.0 * np.cos(index * (2.0 * math.pi / GRID))
    screen = (4.0 * math.pi / GRID) ** 2
    shift = screen + roots[:, None] + roots[None, :]
    spread = np.sqrt(shift + shift * shift / 4.0)
    decay = 1.0 / (1.0 + shift / 2.0 + spread)
    scale = 1.0 / (2.0 * spread * GRID**2)
    mean = np.zeros((1, GRID))
    mean[0, 0] = 2.0 * spread[0, 0] / (GRID * screen)
    chips = np.stack([decay ** (8 * k) for k in range(YS)])
    runs = np.stack([decay**32, decay**64, 1.0 / (1.0 - decay**GRID)])
    as32 = lambda value: np.asarray(value, dtype=np.float32)
    return right, left, as32(decay), as32(scale), as32(mean), as32(chips), as32(runs)


def split(value):
    high = value.astype(BF16)
    low = (value - high.astype(F32)).astype(BF16)
    return high, low


def times_right(value, table):
    full = jnp.dot(jnp.concatenate(split(value), axis=1), table, preferred_element_type=F32)
    return full[:, :GRID] + full[:, GRID:]


def times_left(value, table):
    full = jnp.dot(table, jnp.concatenate(split(value), axis=0), preferred_element_type=F32)
    return full[:GRID] + full[GRID:]


def place():
    spot = lax.axis_index("grid")
    return spot // (YS * CORES), (spot // CORES) % YS, spot % CORES


def quarter_of(which):
    return pl.ds(pl.multiple_of(which * QUARTER, QUARTER), QUARTER)


def array(shape, dtype=F32):
    return jax.ShapeDtypeStruct(tuple(shape), dtype)


HBM = pl.BlockSpec(memory_space=pltpu.HBM)
VMEM = pl.BlockSpec(memory_space=pltpu.VMEM)
SMEM = pl.BlockSpec(memory_space=pltpu.SMEM)


def launch(kernel, token, args, in_specs, out_specs, out_shape, name, limit, grid=(), scratch=(), after=()):
    ins, outs, waits = len(args), len(out_shape), 1 + len(after)
    unread = pl.BlockSpec(memory_space=pl.ANY)

    def ordered(*refs):
        kernel(*refs[:ins], *refs[ins + waits : ins + waits + outs], *refs[ins + waits + outs + 1 :])

    result = pl.pallas_call(
        ordered,
        grid=grid,
        in_specs=[*in_specs, *[unread] * waits],
        out_specs=[*out_specs, unread],
        scratch_shapes=list(scratch),
        out_shape=[*out_shape, array(token.shape)],
        compiler_params=pltpu.CompilerParams(vmem_limit_bytes=limit << 20),
        cost_estimate=pl.CostEstimate(flops=0, bytes_accessed=0, transcendentals=0),
        name=name,
    )(*args, token, *after)
    return result[:-1], result[-1]


def message(pairs):
    return array((pairs * EDGE + 8, GRID))


def pairs_of(ref):
    return ref.shape[0] // EDGE


def copy_all(copies, sems):
    started = []
    for number, (source, target) in enumerate(copies):
        copy = pltpu.make_async_copy(source, target, sems.at[number])
        copy.start()
        started.append(copy)
    for copy in started:
        copy.wait()


def load_kernel(blocks, out, sem):
    copy = pltpu.make_async_copy(blocks, out, sem)
    copy.start()
    copy.wait()


def load(token, blocks):
    (out,), token = launch(
        load_kernel, token, [blocks], [HBM], [VMEM], [array(blocks.shape)], "load", 2,
        scratch=[pltpu.SemaphoreType.DMA],
    )
    return out, token


def pick_kernel(plan, own_a, own_b, index, first, second, sems):
    band_count = lax.axis_size("band")
    band_me = lax.axis_index("band")
    core = place()[2]
    index[0] = plan[0, band_me, 0]
    index[1] = plan[1, (band_me + 2) % band_count, 1]
    index[2] = plan[0, (band_me + 1) % band_count, 1]
    index[3] = plan[1, band_me, 0]
    copies = []
    for step, out in enumerate((first, second)):
        start = index[ROUNDS + step] * SUB + core * HALF
        for source, own in enumerate((own_a, own_b)):
            copies.append((own.at[pl.ds(start, HALF)], out.at[source]))
    copy_all(copies, sems)


def pick(token, plan, own):
    two = array((CORES, HALF, ROWS, GRID))
    outs, token = launch(
        pick_kernel, token, [plan, *own], [SMEM, VMEM, VMEM], [SMEM] + [VMEM] * 2,
        [array((2 * ROUNDS,), jnp.int32), two, two], "pick", 2,
        scratch=[pltpu.SemaphoreType.DMA((2 * CORES,))],
    )
    return *outs, token


def pick_own_kernel(index, own_a, own_b, out, sems):
    copy_all(
        [
            (own.at[pl.ds(index[step] * SUB, SUB)], out.at[step, source])
            for step in range(ROUNDS)
            for source, own in enumerate((own_a, own_b))
        ],
        sems,
    )


def pick_own(token, index, own):
    (out,), token = launch(
        pick_own_kernel, token, [index, *own], [SMEM, VMEM, VMEM], [VMEM],
        [array((ROUNDS, CORES, SUB, ROWS, GRID))], "pick_own", 2,
        scratch=[pltpu.SemaphoreType.DMA((ROUNDS * CORES,))],
    )
    return out, token


def forward_kernel(step, member, own, part, right, left, decay, scale, spec, a, b, c, d, lines):
    outs = (a, b, c, d)
    _, y, core = place()
    j = pl.program_id(0)
    for i in range(SUB):
        for source in range(CORES):
            spot = i * CORES + source
            lines[spot] = times_right(own[step, source, i] * part[source, member + j], right[...])
            half = (core if source == 0 else 1 - core) * PLANES
            for x in range(0, PLANES, 2):
                two = jnp.concatenate(
                    [lines[spot, pl.ds(x + k, GRID, stride=PLANES), :] for k in range(2)], axis=1
                )
                two = times_left(two, left[...])
                for k in range(2):
                    spec[j * SUB + i, half + x + k] = two[:, k * GRID : (k + 1) * GRID] * scale[...]
    for i in range(SUB):
        pair = j * SUB + i
        base = pl.multiple_of(pair * EDGE, EDGE)
        total = spec[pair, 0, 0:1, :]
        for x in range(1, 2 * PLANES):
            total = total + spec[pair, x, 0:1, :]
        for k in range(YS):
            rows = quarter_of((y + k) % YS)
            ratio = decay[rows, :]
            planes = [spec[pair, x, rows, :] for x in range(2 * PLANES)]
            ahead, behind = planes[0], planes[-1]
            for x in range(1, 2 * PLANES):
                ahead = planes[x] + ratio * ahead
                behind = planes[-1 - x] + ratio * behind
            outs[k][pl.ds(base, QUARTER), :] = ahead
            outs[k][pl.ds(base + QUARTER, QUARTER), :] = behind
            outs[k][pl.ds(pairs_of(a) * EDGE + pair, 1), :] = total


def forward(token, step, members, own, part):
    right, left, decay, scale = tables()[:4]
    pairs = len(members) * SUB
    outs, token = launch(
        functools.partial(forward_kernel, step, members[0]),
        token,
        [own, part, right, left, decay, scale],
        [VMEM] * 6,
        [VMEM] * (1 + YS),
        [array((pairs, 2 * PLANES, GRID, GRID))] + [message(pairs)] * YS,
        "forward", 12, grid=(len(members),),
        scratch=[pltpu.VMEM((SUB * CORES, ROWS, GRID), F32)],
    )
    return outs[0], outs[1:], token


def run_kernel(a, b, c, d, chips, out):
    _, y, _ = place()
    rows = quarter_of(y)
    got = (a, b, c, d)
    from_chip = [(y - k + YS) % YS for k in range(YS)]
    ahead = [chips[YS - 1 - chip, rows, :] for chip in from_chip]
    behind = [chips[chip, rows, :] for chip in from_chip]
    for pair in range(pairs_of(out)):
        base = pair * EDGE
        for weights, start in ((ahead, base), (behind, base + QUARTER)):
            at = slice(start, start + QUARTER)
            out[at, :] = sum(got[k][at, :] * weights[k] for k in range(YS))
    at = slice(pairs_of(out) * EDGE, pairs_of(out) * EDGE + 8)
    out[at, :] = sum(got[k][at, :] for k in range(YS))


def two_kernel(mine, other, runs, out):
    z, y, _ = place()
    power = runs[0, quarter_of(y), :]
    odd = (jnp.zeros(power.shape, jnp.int32) + z % 2) == 1
    ones = jnp.ones_like(power)
    first = jnp.where(odd, ones, power)
    second = jnp.where(odd, power, ones)
    for pair in range(pairs_of(out)):
        base = pair * EDGE
        at = slice(base, base + QUARTER)
        out[at, :] = mine[at, :] * first + other[at, :] * second
        at = slice(base + QUARTER, base + 2 * QUARTER)
        out[at, :] = mine[at, :] * second + other[at, :] * first
    at = slice(pairs_of(mine) * EDGE, pairs_of(mine) * EDGE + 8)
    out[at, :] = mine[at, :] + other[at, :]


def edges_kernel(a, b, c, d, near, mine, other, chips, runs, *rest):
    outs, held = rest[:YS], rest[YS]
    z, y, _ = place()
    rows = quarter_of(y)
    got = (a, b, c, d)
    step, run, two, wrap = chips[1, rows, :], runs[0, rows, :], runs[1, rows, :], runs[2, rows, :]
    odd = (jnp.zeros(step.shape, jnp.int32) + z % 2) == 1
    for k in range(YS):
        held[(y - k + YS) % YS] = got[k][...]
    for pair in range(pairs_of(a)):
        base = pair * EDGE
        ahead = slice(base, base + QUARTER)
        behind = slice(base + QUARTER, base + 2 * QUARTER)
        from_left = (other[ahead, :] + two * mine[ahead, :]) * wrap
        from_right = (other[behind, :] + two * mine[behind, :]) * wrap
        from_left = jnp.where(odd, near[ahead, :] + run * from_left, from_left)
        from_right = jnp.where(odd, from_right, near[behind, :] + run * from_right)
        for chip in range(YS):
            chip_ahead = held[chip, ahead, :]
            held[chip, ahead, :] = from_left
            from_left = chip_ahead + step * from_left
        for chip in reversed(range(YS)):
            chip_behind = held[chip, behind, :]
            held[chip, behind, :] = from_right
            from_right = chip_behind + step * from_right
    at = slice(pairs_of(mine) * EDGE, pairs_of(mine) * EDGE + 8)
    total = mine[at, :] + other[at, :]
    for k in range(YS):
        outs[k][...] = held[(y - k + YS) % YS]
        outs[k][at, :] = total


def small(kernel, token, args, count, name, scratch=(), after=()):
    return launch(
        kernel, token, args, [VMEM] * len(args), [VMEM] * count, [array(args[0].shape)] * count, name, 6,
        scratch=scratch, after=after,
    )


def backward_kernel(step, member, prior, extra, spec, a, b, c, d, own, part, right, left, decay, mean, *rest):
    before, (part_out, own_out_a, own_out_b, field, lines) = rest[: prior + extra], rest[prior + extra :]
    j = pl.program_id(0)
    edges = (a, b, c, d)
    _, y, core = place()
    for i in range(SUB):
        pair = j * SUB + i
        base = pl.multiple_of(pair * EDGE, EDGE)
        for k in range(YS):
            rows = quarter_of((y + k) % YS)
            ratio = decay[rows, :]
            planes = [spec[pair, x, rows, :] for x in range(2 * PLANES)]
            ahead = edges[k][pl.ds(base, QUARTER), :]
            behind = edges[k][pl.ds(base + QUARTER, QUARTER), :]
            sums = []
            for x in range(2 * PLANES):
                ahead = planes[x] + ratio * ahead
                sums.append(ahead)
            for x in reversed(range(2 * PLANES)):
                behind = ratio * behind
                field[i, x, rows, :] = sums[x] + behind
                behind = planes[x] + behind
        average = a[pl.ds(pairs_of(a) * EDGE + pair, 1), :] * mean[...]
        for x in range(2 * PLANES):
            field[i, x, 0:1, :] = field[i, x, 0:1, :] - average
    for source, own_out in enumerate((own_out_a, own_out_b)):
        half = (core if source == 0 else 1 - core) * PLANES
        added = None
        for i in range(SUB):
            spot = i * CORES + source
            for x in range(0, PLANES, 2):
                two = jnp.concatenate([field[i, half + x + k] for k in range(2)], axis=1)
                two = times_left(two, left[...])
                for k in range(2):
                    lines[spot, pl.ds(x + k, GRID, stride=PLANES), :] = two[:, k * GRID : (k + 1) * GRID]
            potential = times_right(lines[spot], right[...])
            to_part = potential * own[step, source, i]
            to_own = potential * part[source, member + j]
            added = to_part if added is None else added + to_part
            if prior:
                own_out[0, i] = before[source][0, i] - to_own
            else:
                own_out[0, i] = jnp.where(j == 0, 0.0, own_out[0, i]) - to_own
        part_out[source, j] = -added
    if extra:
        own_out_b[1] = before[prior][0]


def backward(token, step, members, spec, edges, own, part, prior=(), extra=(), after=()):
    right, left, decay, _, mean = tables()[:5]
    args = [spec, *edges, own, part, right, left, decay, mean, *prior, *extra]
    outs, token = launch(
        functools.partial(backward_kernel, step, members[0], len(prior), len(extra)),
        token,
        args,
        [VMEM] * len(args),
        [VMEM] * 3,
        [
            array((CORES, len(members), ROWS, GRID)),
            array((1, SUB, ROWS, GRID)),
            array((1 + len(extra), SUB, ROWS, GRID)),
        ],
        "backward", 12, grid=(len(members),),
        scratch=[
            pltpu.VMEM((SUB, 2 * PLANES, GRID, GRID), F32),
            pltpu.VMEM((SUB * CORES, ROWS, GRID), F32),
        ],
        after=after,
    )
    return outs[0], outs[1:], token


def early_kernel(index, own_first, own_second, swapped, first, first_swapped, same, cross, out):
    core = place()[2]
    for i in range(SUB):
        out[index[0] * SUB + i] = own_first[0, i] + swapped[0, i]
        out[(NSUB - 1 - index[0]) * SUB + i] = jnp.zeros((ROWS, GRID), F32)
    for i in range(SUB):
        band = index[1] * SUB + i
        out[band] = out[band] + (own_second[0, i] + swapped[1, i])
    for part, target in ((same, core), (cross, 1 - core)):
        for member in range(HALF):
            band = index[ROUNDS + 1] * SUB + target * HALF + member
            out[band] = out[band] + part[0, member]
    for part, target in ((first, core), (first_swapped, 1 - core)):
        band = index[ROUNDS] * SUB + target * HALF
        out[band] = out[band] + part[0, 0]


def add_early(token, index, terms):
    (total,), token = launch(
        early_kernel, token, [index, *terms], [SMEM] + [VMEM] * len(terms),
        [VMEM], [array((NSUB * SUB, ROWS, GRID))], "add_early", 4,
    )
    return total, token


def late_kernel(index, total, same, swapped, out, fresh, sems):
    core = place()[2]
    base = index[ROUNDS] * SUB
    other = (NSUB - 1) * SUB - base
    copies = [(total.at[pl.ds(other, SUB)], out.at[pl.ds(other, SUB)])]
    copies += [
        (total.at[pl.ds(base + HALF * k, 1)], out.at[pl.ds(base + HALF * k, 1)]) for k in range(CORES)
    ]
    started = [pltpu.make_async_copy(*copy, sems.at[k]) for k, copy in enumerate(copies)]
    for copy in started:
        copy.start()
    for k, (part, target) in enumerate(((same, core), (swapped, 1 - core))):
        band = base + target * HALF + 1
        fresh[k] = total[band] + part[0, 0]
        copy = pltpu.make_async_copy(
            fresh.at[pl.ds(k, 1)], out.at[pl.ds(band, 1)], sems.at[len(started)]
        )
        copy.start()
        started.append(copy)
    for copy in started:
        copy.wait()


def add_late(token, index, total, terms):
    (total,), token = launch(
        late_kernel, token, [index, total, *terms], [SMEM] + [VMEM] * 3, [HBM],
        [array(total.shape)], "add_late", 4,
        scratch=[pltpu.VMEM((CORES, ROWS, GRID), F32), pltpu.SemaphoreType.DMA((1 + 2 * CORES,))],
    )
    return total


def body(orbitals, plan):
    bands = lax.axis_size("band")
    spots = lax.axis_size("grid")

    def move(value, target):
        pairs = []
        for band in range(bands):
            for spot in range(spots):
                z, y, core = spot // (YS * CORES), (spot // CORES) % YS, spot % CORES
                b2, z2, y2, c2 = target(band, z, y, core)
                pairs.append((band * spots + spot, (b2 % bands) * spots + (z2 * YS + y2 % YS) * CORES + c2))
        return lax.ppermute(value, ("band", "grid"), pairs)

    def swap_cores(value):
        return move(value, lambda b, z, y, c: (b, z, y, 1 - c))

    def shift(value, steps):
        return move(value, lambda b, z, y, c: (b + steps, z, y, c))

    def along_y(messages, sign):
        return [messages[0]] + [
            move(messages[k], lambda b, z, y, c, k=k: (b, z, y + YS + sign * k, c)) for k in range(1, YS)
        ]

    chips, runs = tables()[5:7]
    blocks = orbitals.reshape(NSUB * SUB, PLANES, GRID, GRID).transpose(0, 2, 1, 3)
    blocks = blocks.reshape(NSUB * SUB, ROWS, GRID)
    swapped = swap_cores(blocks)
    held, token = load(jnp.zeros((8, GRID), F32), blocks)
    both = (held, swapped)
    index, *sends, token = pick(token, plan, both)
    parts = [shift(sends[0], 1), shift(sends[1], -2)]
    own, token = pick_own(token, index, both)
    chains = [{} for _ in CHAINS]

    def start(at):
        nonlocal token
        step, members = CHAINS[at]
        chain = chains[at]
        chain["spec"], sums, token = forward(token, step, members, own, parts[step])
        chain["sums"] = along_y(sums, 1)

    def run(at):
        nonlocal token
        chain = chains[at]
        (chain["run"],), token = small(run_kernel, token, [*chain["sums"], chips], 1, "run")
        chain["near"] = move(chain["run"], lambda b, z, y, c: (b, z ^ 1, y, c))

    def two(at):
        nonlocal token
        chain = chains[at]
        (chain["two"],), token = small(two_kernel, token, [chain["run"], chain["near"], runs], 1, "two")
        chain["far"] = move(chain["two"], lambda b, z, y, c: (b, z ^ 2, y, c))

    def edges(at, after=()):
        nonlocal token
        chain = chains[at]
        args = [*chain["sums"], chain["near"], chain["two"], chain["far"], chips, runs]
        outs, token = small(
            edges_kernel, token, args, YS, "edges", [pltpu.VMEM((YS, *chain["run"].shape), F32)], after
        )
        chain["edges"] = along_y(outs, -1)

    def finish(at, prior=(), extra=(), after=()):
        nonlocal token
        step, members = CHAINS[at]
        chain = chains[at]
        terms, sums, token = backward(
            token, step, members, chain["spec"], chain["edges"], own, parts[step], prior, extra, after
        )
        return terms, sums

    second, first, last = range(len(CHAINS))
    start(second)
    run(second)
    start(first)
    two(second)
    start(last)
    run(first)
    run(last)
    edges(second)
    two(first)
    two(last)
    edges(first)
    terms_b, sums_b = finish(second)
    edges(last)
    terms_a, sums_a = finish(first)
    back_a = shift(terms_a, -1)
    terms_a, sums_a = finish(last, sums_a, sums_b[1:], [back_a])
    back_b = [shift(terms_b[:1], 2), move(terms_b[1:], lambda b, z, y, c: (b + 2, z, y, 1 - c))]
    total, token = add_early(
        token, index,
        [sums_a[0], sums_b[0], swap_cores(sums_a[1]), back_a, swap_cores(back_a[1:]), *back_b],
    )
    back_a = shift(terms_a, -1)
    final = [back_a, swap_cores(back_a[1:])]
    total = add_late(token, index, total, final)
    total = total.reshape(NSUB * SUB, GRID, PLANES, GRID).transpose(0, 2, 1, 3)
    return total.reshape(NSUB * SUB, PLANES, GRID * GRID)


def solution(mesh):
    in_specs = (P("band", "grid", None), P())
    out_specs = P("band", "grid", None)
    return jax.shard_map(body, mesh=mesh, in_specs=in_specs, out_specs=out_specs, check_vma=False)
```

```python
import functools
import math

import jax
import jax.numpy as jnp
import ml_dtypes
import numpy as np
from jax import lax
from jax.experimental import pallas as pl
from jax.experimental.pallas import tpu as pltpu
from jax.sharding import PartitionSpec as P

GRID = 128
SUB = 4
NSUB = 2
ROUNDS = 2
CORES = 2
YS = 4
ZS = 4
PLANES = 4
ROWS = GRID * PLANES
HALF = SUB // CORES
QUARTER = GRID // YS
EDGE = 2 * QUARTER
CHAINS = ((1, (0, 1)), (0, (0,)), (0, (1,)))
F32 = jnp.float32
BF16 = jnp.bfloat16


@functools.cache
def tables():
    index = np.arange(GRID, dtype=np.int64)
    angle = (index[:, None] * index[None, :] % GRID) * (2.0 * math.pi / GRID)
    cas = (np.cos(angle) + np.sin(angle)).astype(np.float32)
    high = cas.astype(ml_dtypes.bfloat16)
    low = (cas - high.astype(np.float32)).astype(ml_dtypes.bfloat16)
    zero = np.zeros_like(high)
    right = np.block([[high, low], [high, zero]])
    left = np.block([[high, high], [low, zero]])
    roots = 2.0 - 2.0 * np.cos(index * (2.0 * math.pi / GRID))
    screen = (4.0 * math.pi / GRID) ** 2
    shift = screen + roots[:, None] + roots[None, :]
    spread = np.sqrt(shift + shift * shift / 4.0)
    decay = 1.0 / (1.0 + shift / 2.0 + spread)
    scale = 1.0 / (2.0 * spread * GRID**2)
    mean = np.zeros((1, GRID))
    mean[0, 0] = 2.0 * spread[0, 0] / (GRID * screen)
    chips = np.stack([decay ** (8 * k) for k in range(YS)])
    runs = np.stack([decay**32, decay**64, 1.0 / (1.0 - decay**GRID)])
    as32 = lambda value: np.asarray(value, dtype=np.float32)
    return right, left, as32(decay), as32(scale), as32(mean), as32(chips), as32(runs)


def split(value):
    high = value.astype(BF16)
    low = (value - high.astype(F32)).astype(BF16)
    return high, low


def times_right(value, table):
    full = jnp.dot(jnp.concatenate(split(value), axis=1), table, preferred_element_type=F32)
    return full[:, :GRID] + full[:, GRID:]


def times_left(value, table):
    full = jnp.dot(table, jnp.concatenate(split(value), axis=0), preferred_element_type=F32)
    return full[:GRID] + full[GRID:]


def place():
    spot = lax.axis_index("grid")
    return spot // (YS * CORES), (spot // CORES) % YS, spot % CORES


def quarter_of(which):
    return pl.ds(pl.multiple_of(which * QUARTER, QUARTER), QUARTER)


def array(shape, dtype=F32):
    return jax.ShapeDtypeStruct(tuple(shape), dtype)


HBM = pl.BlockSpec(memory_space=pltpu.HBM)
VMEM = pl.BlockSpec(memory_space=pltpu.VMEM)
SMEM = pl.BlockSpec(memory_space=pltpu.SMEM)


def launch(kernel, token, args, in_specs, out_specs, out_shape, name, limit, grid=(), scratch=(), after=(), work=0):
    tokens = [] if token is None else [token]
    ins, outs, waits = len(args), len(out_shape), len(tokens) + len(after)
    unread = pl.BlockSpec(memory_space=pl.ANY)

    def ordered(*refs):
        kernel(*refs[:ins], *refs[ins + waits : ins + waits + outs], *refs[ins + waits + outs + 1 :])

    result = pl.pallas_call(
        ordered,
        grid=grid,
        in_specs=[*in_specs, *[unread] * waits],
        out_specs=[*out_specs, unread],
        scratch_shapes=list(scratch),
        out_shape=[*out_shape, array((8, GRID))],
        compiler_params=pltpu.CompilerParams(vmem_limit_bytes=limit << 20),
        cost_estimate=pl.CostEstimate(flops=work, bytes_accessed=work // 256, transcendentals=0),
        name=name,
    )(*args, *tokens, *after)
    return result[:-1], result[-1]


def message(pairs):
    return array((pairs * EDGE + 8, GRID))


def pairs_of(ref):
    return ref.shape[0] // EDGE


def copy_all(copies, sems):
    started = []
    for number, (source, target) in enumerate(copies):
        copy = pltpu.make_async_copy(source, target, sems.at[number])
        copy.start()
        started.append(copy)
    for copy in started:
        copy.wait()


def pick_kernel(plan, own_a, own_b, index, first, second, sems):
    band_count = lax.axis_size("band")
    band_me = lax.axis_index("band")
    core = place()[2]
    index[0] = plan[0, band_me, 0]
    index[1] = plan[1, (band_me + 2) % band_count, 1]
    index[2] = plan[0, (band_me + 1) % band_count, 1]
    index[3] = plan[1, band_me, 0]
    copies = []
    for step, out in enumerate((first, second)):
        start = index[ROUNDS + step] * SUB + core * HALF
        for source, own in enumerate((own_a, own_b)):
            copies.append((own.at[pl.ds(start, HALF)], out.at[source]))
    copy_all(copies, sems)


def pick(plan, own):
    two = array((CORES, HALF, ROWS, GRID))
    outs, token = launch(
        pick_kernel, None, [plan, *own], [SMEM, HBM, VMEM], [SMEM] + [VMEM] * 2,
        [array((2 * ROUNDS,), jnp.int32), two, two], "pick", 2,
        scratch=[pltpu.SemaphoreType.DMA((2 * CORES,))],
    )
    return *outs, token


def pick_own_kernel(index, own_a, own_b, out, sems):
    copy_all(
        [
            (own.at[pl.ds(index[step] * SUB, SUB)], out.at[step, source])
            for step in range(ROUNDS)
            for source, own in enumerate((own_a, own_b))
        ],
        sems,
    )


def pick_own(token, index, own):
    (out,), token = launch(
        pick_own_kernel, token, [index, *own], [SMEM, HBM, VMEM], [VMEM],
        [array((ROUNDS, CORES, SUB, ROWS, GRID))], "pick_own", 2,
        scratch=[pltpu.SemaphoreType.DMA((ROUNDS * CORES,))],
    )
    return out, token


def forward_kernel(step, member, own, part, right, left, decay, scale, spec, a, b, c, d, lines):
    outs = (a, b, c, d)
    _, y, core = place()
    j = pl.program_id(0)
    for i in range(SUB):
        for source in range(CORES):
            spot = i * CORES + source
            lines[spot] = times_right(own[step, source, i] * part[source, member + j], right[...])
            half = (core if source == 0 else 1 - core) * PLANES
            for x in range(0, PLANES, 2):
                two = jnp.concatenate(
                    [lines[spot, pl.ds(x + k, GRID, stride=PLANES), :] for k in range(2)], axis=1
                )
                two = times_left(two, left[...])
                for k in range(2):
                    spec[j * SUB + i, half + x + k] = two[:, k * GRID : (k + 1) * GRID] * scale[...]
    for i in range(SUB):
        pair = j * SUB + i
        base = pl.multiple_of(pair * EDGE, EDGE)
        total = spec[pair, 0, 0:1, :]
        for x in range(1, 2 * PLANES):
            total = total + spec[pair, x, 0:1, :]
        for k in range(YS):
            rows = quarter_of((y + k) % YS)
            ratio = decay[rows, :]
            planes = [spec[pair, x, rows, :] for x in range(2 * PLANES)]
            ahead, behind = planes[0], planes[-1]
            for x in range(1, 2 * PLANES):
                ahead = planes[x] + ratio * ahead
                behind = planes[-1 - x] + ratio * behind
            outs[k][pl.ds(base, QUARTER), :] = ahead
            outs[k][pl.ds(base + QUARTER, QUARTER), :] = behind
            outs[k][pl.ds(pairs_of(a) * EDGE + pair, 1), :] = total


def forward(token, step, members, own, part):
    right, left, decay, scale = tables()[:4]
    pairs = len(members) * SUB
    outs, token = launch(
        functools.partial(forward_kernel, step, members[0]),
        token,
        [own, part, right, left, decay, scale],
        [VMEM] * 6,
        [VMEM] * (1 + YS),
        [array((pairs, 2 * PLANES, GRID, GRID))] + [message(pairs)] * YS,
        "forward", 12, grid=(len(members),),
        scratch=[pltpu.VMEM((SUB * CORES, ROWS, GRID), F32)],
    )
    return outs[0], outs[1:], token


def run_kernel(a, b, c, d, chips, out):
    _, y, _ = place()
    rows = quarter_of(y)
    got = (a, b, c, d)
    from_chip = [(y - k + YS) % YS for k in range(YS)]
    ahead = [chips[YS - 1 - chip, rows, :] for chip in from_chip]
    behind = [chips[chip, rows, :] for chip in from_chip]
    for pair in range(pairs_of(out)):
        base = pair * EDGE
        for weights, start in ((ahead, base), (behind, base + QUARTER)):
            at = slice(start, start + QUARTER)
            out[at, :] = sum(got[k][at, :] * weights[k] for k in range(YS))
    at = slice(pairs_of(out) * EDGE, pairs_of(out) * EDGE + 8)
    out[at, :] = sum(got[k][at, :] for k in range(YS))


def two_kernel(mine, other, runs, out):
    z, y, _ = place()
    power = runs[0, quarter_of(y), :]
    odd = (jnp.zeros(power.shape, jnp.int32) + z % 2) == 1
    ones = jnp.ones_like(power)
    first = jnp.where(odd, ones, power)
    second = jnp.where(odd, power, ones)
    for pair in range(pairs_of(out)):
        base = pair * EDGE
        at = slice(base, base + QUARTER)
        out[at, :] = mine[at, :] * first + other[at, :] * second
        at = slice(base + QUARTER, base + 2 * QUARTER)
        out[at, :] = mine[at, :] * second + other[at, :] * first
    at = slice(pairs_of(mine) * EDGE, pairs_of(mine) * EDGE + 8)
    out[at, :] = mine[at, :] + other[at, :]


def edges_kernel(a, b, c, d, near, mine, other, chips, runs, *rest):
    outs, held = rest[:YS], rest[YS]
    z, y, _ = place()
    rows = quarter_of(y)
    got = (a, b, c, d)
    step, run, two, wrap = chips[1, rows, :], runs[0, rows, :], runs[1, rows, :], runs[2, rows, :]
    odd = (jnp.zeros(step.shape, jnp.int32) + z % 2) == 1
    for k in range(YS):
        held[(y - k + YS) % YS] = got[k][...]
    for pair in range(pairs_of(a)):
        base = pair * EDGE
        ahead = slice(base, base + QUARTER)
        behind = slice(base + QUARTER, base + 2 * QUARTER)
        from_left = (other[ahead, :] + two * mine[ahead, :]) * wrap
        from_right = (other[behind, :] + two * mine[behind, :]) * wrap
        from_left = jnp.where(odd, near[ahead, :] + run * from_left, from_left)
        from_right = jnp.where(odd, from_right, near[behind, :] + run * from_right)
        for chip in range(YS):
            chip_ahead = held[chip, ahead, :]
            held[chip, ahead, :] = from_left
            from_left = chip_ahead + step * from_left
        for chip in reversed(range(YS)):
            chip_behind = held[chip, behind, :]
            held[chip, behind, :] = from_right
            from_right = chip_behind + step * from_right
    at = slice(pairs_of(mine) * EDGE, pairs_of(mine) * EDGE + 8)
    total = mine[at, :] + other[at, :]
    for k in range(YS):
        outs[k][...] = held[(y - k + YS) % YS]
        outs[k][at, :] = total


def small(kernel, token, args, count, name, scratch=(), after=()):
    return launch(
        kernel, token, args, [VMEM] * len(args), [VMEM] * count, [array(args[0].shape)] * count, name, 6,
        scratch=scratch, after=after,
    )


def backward_kernel(step, member, prior, extra, spec, a, b, c, d, own, part, right, left, decay, mean, *rest):
    before, (part_out, own_out_a, own_out_b, field, lines) = rest[: prior + extra], rest[prior + extra :]
    j = pl.program_id(0)
    edges = (a, b, c, d)
    _, y, core = place()
    for i in range(SUB):
        pair = j * SUB + i
        base = pl.multiple_of(pair * EDGE, EDGE)
        for k in range(YS):
            rows = quarter_of((y + k) % YS)
            ratio = decay[rows, :]
            planes = [spec[pair, x, rows, :] for x in range(2 * PLANES)]
            ahead = edges[k][pl.ds(base, QUARTER), :]
            behind = edges[k][pl.ds(base + QUARTER, QUARTER), :]
            sums = []
            for x in range(2 * PLANES):
                ahead = planes[x] + ratio * ahead
                sums.append(ahead)
            for x in reversed(range(2 * PLANES)):
                behind = ratio * behind
                field[i, x, rows, :] = sums[x] + behind
                behind = planes[x] + behind
        average = a[pl.ds(pairs_of(a) * EDGE + pair, 1), :] * mean[...]
        for x in range(2 * PLANES):
            field[i, x, 0:1, :] = field[i, x, 0:1, :] - average
    for source, own_out in enumerate((own_out_a, own_out_b)):
        half = (core if source == 0 else 1 - core) * PLANES
        added = None
        for i in range(SUB):
            spot = i * CORES + source
            for x in range(0, PLANES, 2):
                two = jnp.concatenate([field[i, half + x + k] for k in range(2)], axis=1)
                two = times_left(two, left[...])
                for k in range(2):
                    lines[spot, pl.ds(x + k, GRID, stride=PLANES), :] = two[:, k * GRID : (k + 1) * GRID]
            potential = times_right(lines[spot], right[...])
            to_part = potential * own[step, source, i]
            to_own = potential * part[source, member + j]
            added = to_part if added is None else added + to_part
            if prior:
                own_out[i] = before[source][i] - to_own
            else:
                own_out[i] = jnp.where(j == 0, 0.0, own_out[i]) - to_own
        part_out[source, j] = -added
    if extra:
        own_out_b[SUB : 2 * SUB] = before[prior][...]


def backward(token, step, members, spec, edges, own, part, prior=(), extra=()):
    right, left, decay, _, mean = tables()[:5]
    args = [spec, *edges, own, part, right, left, decay, mean, *prior, *extra]
    outs, token = launch(
        functools.partial(backward_kernel, step, members[0], len(prior), len(extra)),
        token,
        args,
        [VMEM] * len(args),
        [VMEM] * 3,
        [
            array((CORES, len(members), ROWS, GRID)),
            array((SUB, ROWS, GRID)),
            array((2 * SUB if extra else SUB, ROWS, GRID)),
        ],
        "backward", 12, grid=(len(members),),
        scratch=[
            pltpu.VMEM((SUB, 2 * PLANES, GRID, GRID), F32),
            pltpu.VMEM((SUB * CORES, ROWS, GRID), F32),
        ],
    )
    return outs[0], outs[1:], token


def early_kernel(index, own_first, own_second, out):
    for i in range(SUB):
        out[index[0] * SUB + i] = own_first[i]
        out[(NSUB - 1 - index[0]) * SUB + i] = jnp.zeros((ROWS, GRID), F32)
    for i in range(SUB):
        band = index[1] * SUB + i
        out[band] = out[band] + own_second[i]


def add_early(token, index, terms):
    (total,), token = launch(
        early_kernel, token, [index, *terms], [SMEM] + [VMEM] * len(terms),
        [VMEM], [array((NSUB * SUB, ROWS, GRID))], "add_early", 4, work=40_000_000_000,
    )
    return total, token


def middle_kernel(index, total, swapped, same, cross, first_same, first_cross, out):
    core = place()[2]
    for band in range(NSUB * SUB):
        out[band] = total[band]
    for step in range(ROUNDS):
        for i in range(SUB):
            band = index[step] * SUB + i
            out[band] = out[band] + swapped[step * SUB + i]
    for part, target in ((same, core), (cross, 1 - core)):
        for member in range(HALF):
            band = index[ROUNDS + 1] * SUB + target * HALF + member
            out[band] = out[band] + part[0, member]
    for part, target in ((first_same, core), (first_cross, 1 - core)):
        band = index[ROUNDS] * SUB + target * HALF
        out[band] = out[band] + part[0, 0]


def add_middle(token, index, terms):
    (total,), token = launch(
        middle_kernel, token, [index, *terms], [SMEM] + [VMEM] * len(terms),
        [VMEM], [array((NSUB * SUB, ROWS, GRID))], "add_middle", 4,
    )
    return total, token


def late_kernel(index, total, same, cross, out, fresh, sems):
    core = place()[2]
    base = index[ROUNDS] * SUB
    other = (NSUB - 1) * SUB - base
    copies = [(total.at[pl.ds(other, SUB)], out.at[pl.ds(other, SUB)])]
    copies += [
        (total.at[pl.ds(base + HALF * k, 1)], out.at[pl.ds(base + HALF * k, 1)]) for k in range(CORES)
    ]
    started = [pltpu.make_async_copy(*copy, sems.at[k]) for k, copy in enumerate(copies)]
    for copy in started:
        copy.start()
    for k, (part, target) in enumerate(((same, core), (cross, 1 - core))):
        band = base + target * HALF + 1
        fresh[k] = total[band] + part[0, 0]
        copy = pltpu.make_async_copy(
            fresh.at[pl.ds(k, 1)], out.at[pl.ds(band, 1)], sems.at[len(started)]
        )
        copy.start()
        started.append(copy)
    for copy in started:
        copy.wait()


def add_late(token, index, total, terms):
    (total,), token = launch(
        late_kernel, token, [index, total, *terms], [SMEM] + [VMEM] * 3, [HBM],
        [array(total.shape)], "add_late", 4,
        scratch=[pltpu.VMEM((CORES, ROWS, GRID), F32), pltpu.SemaphoreType.DMA((1 + 2 * CORES,))],
    )
    return total


def body(orbitals, plan):
    bands = lax.axis_size("band")
    spots = lax.axis_size("grid")

    def move(value, target):
        pairs = []
        for band in range(bands):
            for spot in range(spots):
                z, y, core = spot // (YS * CORES), (spot // CORES) % YS, spot % CORES
                b2, z2, y2, c2 = target(band, z, y, core)
                pairs.append((band * spots + spot, (b2 % bands) * spots + (z2 * YS + y2 % YS) * CORES + c2))
        return lax.ppermute(value, ("band", "grid"), pairs)

    def swap_cores(value):
        return move(value, lambda b, z, y, c: (b, z, y, 1 - c))

    def shift(value, steps):
        return move(value, lambda b, z, y, c: (b + steps, z, y, c))

    def there_and_across(values, steps):
        return [shift(values[0], steps), move(values[1], lambda b, z, y, c: (b + steps, z, y, 1 - c))]

    def along_y(messages, sign):
        return [messages[0]] + [
            move(messages[k], lambda b, z, y, c, k=k: (b, z, y + YS + sign * k, c)) for k in range(1, YS)
        ]

    chips, runs = tables()[5:7]
    blocks = orbitals.reshape(NSUB * SUB, PLANES, GRID, GRID).transpose(0, 2, 1, 3)
    blocks = blocks.reshape(NSUB * SUB, ROWS, GRID)
    both = (blocks, swap_cores(blocks))
    index, *sends, token = pick(plan, both)
    parts = [shift(sends[0], 1), shift(sends[1], -2)]
    own, token = pick_own(token, index, both)
    chains = [{} for _ in CHAINS]

    def start(at):
        nonlocal token
        step, members = CHAINS[at]
        chain = chains[at]
        chain["spec"], sums, token = forward(token, step, members, own, parts[step])
        chain["sums"] = along_y(sums, 1)

    def run(at, after=()):
        nonlocal token
        chain = chains[at]
        (chain["run"],), token = small(run_kernel, token, [*chain["sums"], chips], 1, "run", after=after)
        chain["near"] = move(chain["run"], lambda b, z, y, c: (b, z ^ 1, y, c))

    def two(at):
        nonlocal token
        chain = chains[at]
        (chain["two"],), token = small(two_kernel, token, [chain["run"], chain["near"], runs], 1, "two")
        chain["far"] = move(chain["two"], lambda b, z, y, c: (b, z ^ 2, y, c))

    def edges(at, after=()):
        nonlocal token
        chain = chains[at]
        args = [*chain["sums"], chain["near"], chain["two"], chain["far"], chips, runs]
        outs, token = small(
            edges_kernel, token, args, YS, "edges", [pltpu.VMEM((YS, *chain["run"].shape), F32)], after
        )
        chain["edges"] = along_y(outs, -1)

    def finish(at, prior=(), extra=()):
        nonlocal token
        step, members = CHAINS[at]
        chain = chains[at]
        terms, sums, token = backward(
            token, step, members, chain["spec"], chain["edges"], own, parts[step], prior, extra
        )
        return terms, sums

    second, first, last = range(len(CHAINS))
    start(second)
    run(second)
    start(first)
    two(second)
    start(last)
    run(first)
    run(last)
    edges(second)
    two(first)
    two(last)
    edges(first)
    terms_b, sums_b = finish(second)
    edges(last)
    terms_a, sums_a = finish(first)
    back_a = shift(terms_a, -1)
    terms_a, sums_a = finish(last, sums_a, sums_b[1:])
    final = there_and_across((terms_a[:1], terms_a[1:]), -1)
    back_b = there_and_across((terms_b[:1], terms_b[1:]), 2)
    total, token = add_early(token, index, [sums_a[0], sums_b[0]])
    total, token = add_middle(
        token, index, [total, swap_cores(sums_a[1]), *back_b, back_a, swap_cores(back_a[1:])]
    )
    total = add_late(token, index, total, final)
    total = total.reshape(NSUB * SUB, GRID, PLANES, GRID).transpose(0, 2, 1, 3)
    return total.reshape(NSUB * SUB, PLANES, GRID * GRID)


def solution(mesh):
    in_specs = (P("band", "grid", None), P())
    out_specs = P("band", "grid", None)
    return jax.shard_map(body, mesh=mesh, in_specs=in_specs, out_specs=out_specs, check_vma=False)
```

```python
import functools
import math

import jax
import jax.numpy as jnp
import ml_dtypes
import numpy as np
from jax import lax
from jax.experimental import pallas as pl
from jax.experimental.pallas import tpu as pltpu
from jax.sharding import PartitionSpec as P

GRID = 128
SUB = 4
NSUB = 2
ROUNDS = 2
CORES = 2
YS = 4
ZS = 4
PLANES = 4
ROWS = GRID * PLANES
HALF = SUB // CORES
QUARTER = GRID // YS
EDGE = 2 * QUARTER
CHAINS = ((1, (0, 1)), (0, (0,)), (0, (1,)))
F32 = jnp.float32
BF16 = jnp.bfloat16


@functools.cache
def tables():
    index = np.arange(GRID, dtype=np.int64)
    angle = (index[:, None] * index[None, :] % GRID) * (2.0 * math.pi / GRID)
    cas = (np.cos(angle) + np.sin(angle)).astype(np.float32)
    high = cas.astype(ml_dtypes.bfloat16)
    low = (cas - high.astype(np.float32)).astype(ml_dtypes.bfloat16)
    zero = np.zeros_like(high)
    right = np.block([[high, low], [high, zero]])
    left = np.block([[high, high], [low, zero]])
    roots = 2.0 - 2.0 * np.cos(index * (2.0 * math.pi / GRID))
    screen = (4.0 * math.pi / GRID) ** 2
    shift = screen + roots[:, None] + roots[None, :]
    spread = np.sqrt(shift + shift * shift / 4.0)
    decay = 1.0 / (1.0 + shift / 2.0 + spread)
    scale = 1.0 / (2.0 * spread * GRID**2)
    mean = np.zeros((1, GRID))
    mean[0, 0] = 2.0 * spread[0, 0] / (GRID * screen)
    chips = np.stack([decay ** (8 * k) for k in range(YS)])
    runs = np.stack([decay**32, decay**64, 1.0 / (1.0 - decay**GRID)])
    as32 = lambda value: np.asarray(value, dtype=np.float32)
    return right, left, as32(decay), as32(scale), as32(mean), as32(chips), as32(runs)


def split(value):
    high = value.astype(BF16)
    low = (value - high.astype(F32)).astype(BF16)
    return high, low


def times_right(value, table):
    full = jnp.dot(jnp.concatenate(split(value), axis=1), table, preferred_element_type=F32)
    return full[:, :GRID] + full[:, GRID:]


def times_left(value, table):
    full = jnp.dot(table, jnp.concatenate(split(value), axis=0), preferred_element_type=F32)
    return full[:GRID] + full[GRID:]


def place():
    spot = lax.axis_index("grid")
    return spot // (YS * CORES), (spot // CORES) % YS, spot % CORES


def quarter_of(which):
    return pl.ds(pl.multiple_of(which * QUARTER, QUARTER), QUARTER)


def array(shape, dtype=F32):
    return jax.ShapeDtypeStruct(tuple(shape), dtype)


HBM = pl.BlockSpec(memory_space=pltpu.HBM)
VMEM = pl.BlockSpec(memory_space=pltpu.VMEM)
SMEM = pl.BlockSpec(memory_space=pltpu.SMEM)


def launch(kernel, token, args, in_specs, out_specs, out_shape, name, limit, grid=(), scratch=(), after=(), work=0):
    tokens = [] if token is None else [token]
    ins, outs, waits = len(args), len(out_shape), len(tokens) + len(after)
    unread = pl.BlockSpec(memory_space=pl.ANY)

    def ordered(*refs):
        kernel(*refs[:ins], *refs[ins + waits : ins + waits + outs], *refs[ins + waits + outs + 1 :])

    result = pl.pallas_call(
        ordered,
        grid=grid,
        in_specs=[*in_specs, *[unread] * waits],
        out_specs=[*out_specs, unread],
        scratch_shapes=list(scratch),
        out_shape=[*out_shape, array((8, GRID))],
        compiler_params=pltpu.CompilerParams(vmem_limit_bytes=limit << 20),
        cost_estimate=pl.CostEstimate(flops=work, bytes_accessed=work // 256, transcendentals=0),
        name=name,
    )(*args, *tokens, *after)
    return result[:-1], result[-1]


def message(pairs):
    return array((pairs * EDGE + 8, GRID))


def pairs_of(ref):
    return ref.shape[0] // EDGE


def copy_all(copies, sems):
    started = []
    for number, (source, target) in enumerate(copies):
        copy = pltpu.make_async_copy(source, target, sems.at[number])
        copy.start()
        started.append(copy)
    for copy in started:
        copy.wait()


def pick_kernel(plan, own_a, own_b, index, first, second, sems):
    band_count = lax.axis_size("band")
    band_me = lax.axis_index("band")
    core = place()[2]
    index[0] = plan[0, band_me, 0]
    index[1] = plan[1, (band_me + 2) % band_count, 1]
    index[2] = plan[0, (band_me + 1) % band_count, 1]
    index[3] = plan[1, band_me, 0]
    copies = []
    for step, out in enumerate((first, second)):
        start = index[ROUNDS + step] * SUB + core * HALF
        for source, own in enumerate((own_a, own_b)):
            copies.append((own.at[pl.ds(start, HALF)], out.at[source]))
    copy_all(copies, sems)


def pick(plan, own):
    two = array((CORES, HALF, ROWS, GRID))
    outs, token = launch(
        pick_kernel, None, [plan, *own], [SMEM, HBM, VMEM], [SMEM] + [VMEM] * 2,
        [array((2 * ROUNDS,), jnp.int32), two, two], "pick", 2,
        scratch=[pltpu.SemaphoreType.DMA((2 * CORES,))],
    )
    return *outs, token


def pick_own_kernel(index, own_a, own_b, out, sems):
    copy_all(
        [
            (own.at[pl.ds(index[step] * SUB, SUB)], out.at[step, source])
            for step in range(ROUNDS)
            for source, own in enumerate((own_a, own_b))
        ],
        sems,
    )


def pick_own(token, index, own):
    (out,), token = launch(
        pick_own_kernel, token, [index, *own], [SMEM, HBM, VMEM], [VMEM],
        [array((ROUNDS, CORES, SUB, ROWS, GRID))], "pick_own", 2,
        scratch=[pltpu.SemaphoreType.DMA((ROUNDS * CORES,))],
    )
    return out, token


def forward_kernel(step, member, own, part, right, left, decay, scale, spec, a, b, c, d, lines):
    outs = (a, b, c, d)
    _, y, core = place()
    j = pl.program_id(0)
    for i in range(SUB):
        for source in range(CORES):
            spot = i * CORES + source
            lines[spot] = times_right(own[step, source, i] * part[source, member + j], right[...])
            half = (core if source == 0 else 1 - core) * PLANES
            for x in range(0, PLANES, 2):
                two = jnp.concatenate(
                    [lines[spot, pl.ds(x + k, GRID, stride=PLANES), :] for k in range(2)], axis=1
                )
                two = times_left(two, left[...])
                for k in range(2):
                    spec[j * SUB + i, half + x + k] = two[:, k * GRID : (k + 1) * GRID] * scale[...]
    for i in range(SUB):
        pair = j * SUB + i
        base = pl.multiple_of(pair * EDGE, EDGE)
        total = spec[pair, 0, 0:1, :]
        for x in range(1, 2 * PLANES):
            total = total + spec[pair, x, 0:1, :]
        for k in range(YS):
            rows = quarter_of((y + k) % YS)
            ratio = decay[rows, :]
            planes = [spec[pair, x, rows, :] for x in range(2 * PLANES)]
            ahead, behind = planes[0], planes[-1]
            for x in range(1, 2 * PLANES):
                ahead = planes[x] + ratio * ahead
                behind = planes[-1 - x] + ratio * behind
            outs[k][pl.ds(base, QUARTER), :] = ahead
            outs[k][pl.ds(base + QUARTER, QUARTER), :] = behind
            outs[k][pl.ds(pairs_of(a) * EDGE + pair, 1), :] = total


def forward(token, step, members, own, part):
    right, left, decay, scale = tables()[:4]
    pairs = len(members) * SUB
    outs, token = launch(
        functools.partial(forward_kernel, step, members[0]),
        token,
        [own, part, right, left, decay, scale],
        [VMEM] * 6,
        [VMEM] * (1 + YS),
        [array((pairs, 2 * PLANES, GRID, GRID))] + [message(pairs)] * YS,
        "forward", 12, grid=(len(members),),
        scratch=[pltpu.VMEM((SUB * CORES, ROWS, GRID), F32)],
    )
    return outs[0], outs[1:], token


def run_kernel(a, b, c, d, chips, out):
    _, y, _ = place()
    rows = quarter_of(y)
    got = (a, b, c, d)
    from_chip = [(y - k + YS) % YS for k in range(YS)]
    ahead = [chips[YS - 1 - chip, rows, :] for chip in from_chip]
    behind = [chips[chip, rows, :] for chip in from_chip]
    for pair in range(pairs_of(out)):
        base = pair * EDGE
        for weights, start in ((ahead, base), (behind, base + QUARTER)):
            at = slice(start, start + QUARTER)
            out[at, :] = sum(got[k][at, :] * weights[k] for k in range(YS))
    at = slice(pairs_of(out) * EDGE, pairs_of(out) * EDGE + 8)
    out[at, :] = sum(got[k][at, :] for k in range(YS))


def two_kernel(mine, other, runs, out):
    z, y, _ = place()
    power = runs[0, quarter_of(y), :]
    odd = (jnp.zeros(power.shape, jnp.int32) + z % 2) == 1
    ones = jnp.ones_like(power)
    first = jnp.where(odd, ones, power)
    second = jnp.where(odd, power, ones)
    for pair in range(pairs_of(out)):
        base = pair * EDGE
        at = slice(base, base + QUARTER)
        out[at, :] = mine[at, :] * first + other[at, :] * second
        at = slice(base + QUARTER, base + 2 * QUARTER)
        out[at, :] = mine[at, :] * second + other[at, :] * first
    at = slice(pairs_of(mine) * EDGE, pairs_of(mine) * EDGE + 8)
    out[at, :] = mine[at, :] + other[at, :]


def edges_kernel(a, b, c, d, near, mine, other, chips, runs, *rest):
    outs, held = rest[:YS], rest[YS]
    z, y, _ = place()
    rows = quarter_of(y)
    got = (a, b, c, d)
    step, run, two, wrap = chips[1, rows, :], runs[0, rows, :], runs[1, rows, :], runs[2, rows, :]
    odd = (jnp.zeros(step.shape, jnp.int32) + z % 2) == 1
    for k in range(YS):
        held[(y - k + YS) % YS] = got[k][...]
    for pair in range(pairs_of(a)):
        base = pair * EDGE
        ahead = slice(base, base + QUARTER)
        behind = slice(base + QUARTER, base + 2 * QUARTER)
        from_left = (other[ahead, :] + two * mine[ahead, :]) * wrap
        from_right = (other[behind, :] + two * mine[behind, :]) * wrap
        from_left = jnp.where(odd, near[ahead, :] + run * from_left, from_left)
        from_right = jnp.where(odd, from_right, near[behind, :] + run * from_right)
        for chip in range(YS):
            chip_ahead = held[chip, ahead, :]
            held[chip, ahead, :] = from_left
            from_left = chip_ahead + step * from_left
        for chip in reversed(range(YS)):
            chip_behind = held[chip, behind, :]
            held[chip, behind, :] = from_right
            from_right = chip_behind + step * from_right
    at = slice(pairs_of(mine) * EDGE, pairs_of(mine) * EDGE + 8)
    total = mine[at, :] + other[at, :]
    for k in range(YS):
        outs[k][...] = held[(y - k + YS) % YS]
        outs[k][at, :] = total


def small(kernel, token, args, count, name, scratch=(), after=()):
    return launch(
        kernel, token, args, [VMEM] * len(args), [VMEM] * count, [array(args[0].shape)] * count, name, 6,
        scratch=scratch, after=after,
    )


def backward_kernel(step, member, prior, extra, spec, a, b, c, d, own, part, right, left, decay, mean, *rest):
    before, (part_out, own_out_a, own_out_b, field, lines) = rest[: prior + extra], rest[prior + extra :]
    j = pl.program_id(0)
    edges = (a, b, c, d)
    _, y, core = place()
    for i in range(SUB):
        pair = j * SUB + i
        base = pl.multiple_of(pair * EDGE, EDGE)
        for k in range(YS):
            rows = quarter_of((y + k) % YS)
            ratio = decay[rows, :]
            planes = [spec[pair, x, rows, :] for x in range(2 * PLANES)]
            ahead = edges[k][pl.ds(base, QUARTER), :]
            behind = edges[k][pl.ds(base + QUARTER, QUARTER), :]
            sums = []
            for x in range(2 * PLANES):
                ahead = planes[x] + ratio * ahead
                sums.append(ahead)
            for x in reversed(range(2 * PLANES)):
                behind = ratio * behind
                field[i, x, rows, :] = sums[x] + behind
                behind = planes[x] + behind
        average = a[pl.ds(pairs_of(a) * EDGE + pair, 1), :] * mean[...]
        for x in range(2 * PLANES):
            field[i, x, 0:1, :] = field[i, x, 0:1, :] - average
    for source, own_out in enumerate((own_out_a, own_out_b)):
        half = (core if source == 0 else 1 - core) * PLANES
        added = None
        for i in range(SUB):
            spot = i * CORES + source
            for x in range(0, PLANES, 2):
                two = jnp.concatenate([field[i, half + x + k] for k in range(2)], axis=1)
                two = times_left(two, left[...])
                for k in range(2):
                    lines[spot, pl.ds(x + k, GRID, stride=PLANES), :] = two[:, k * GRID : (k + 1) * GRID]
            potential = times_right(lines[spot], right[...])
            to_part = potential * own[step, source, i]
            to_own = potential * part[source, member + j]
            added = to_part if added is None else added + to_part
            if prior:
                own_out[i] = before[source][i] - to_own
            else:
                own_out[i] = jnp.where(j == 0, 0.0, own_out[i]) - to_own
        part_out[source, j] = -added
    if extra:
        own_out_b[SUB : 2 * SUB] = before[prior][...]


def backward(token, step, members, spec, edges, own, part, prior=(), extra=(), after=()):
    right, left, decay, _, mean = tables()[:5]
    args = [spec, *edges, own, part, right, left, decay, mean, *prior, *extra]
    outs, token = launch(
        functools.partial(backward_kernel, step, members[0], len(prior), len(extra)),
        token,
        args,
        [VMEM] * len(args),
        [VMEM] * 3,
        [
            array((CORES, len(members), ROWS, GRID)),
            array((SUB, ROWS, GRID)),
            array((2 * SUB if extra else SUB, ROWS, GRID)),
        ],
        "backward", 12, grid=(len(members),),
        scratch=[
            pltpu.VMEM((SUB, 2 * PLANES, GRID, GRID), F32),
            pltpu.VMEM((SUB * CORES, ROWS, GRID), F32),
        ],
        after=after,
    )
    return outs[0], outs[1:], token


def early_kernel(index, own_first, own_second, out):
    for i in range(SUB):
        out[index[0] * SUB + i] = own_first[i]
        out[(NSUB - 1 - index[0]) * SUB + i] = jnp.zeros((ROWS, GRID), F32)
    for i in range(SUB):
        band = index[1] * SUB + i
        out[band] = out[band] + own_second[i]


def add_early(token, index, terms):
    (total,), token = launch(
        early_kernel, token, [index, *terms], [SMEM] + [VMEM] * len(terms),
        [VMEM], [array((NSUB * SUB, ROWS, GRID))], "add_early", 4, work=40_000_000_000,
    )
    return total, token


def middle_kernel(index, total, swapped, same, cross, first_same, first_cross, out):
    core = place()[2]
    for band in range(NSUB * SUB):
        out[band] = total[band]
    for step in range(ROUNDS):
        for i in range(SUB):
            band = index[step] * SUB + i
            out[band] = out[band] + swapped[step * SUB + i]
    for part, target in ((same, core), (cross, 1 - core)):
        for member in range(HALF):
            band = index[ROUNDS + 1] * SUB + target * HALF + member
            out[band] = out[band] + part[0, member]
    for part, target in ((first_same, core), (first_cross, 1 - core)):
        band = index[ROUNDS] * SUB + target * HALF
        out[band] = out[band] + part[0, 0]


def add_middle(token, index, terms):
    (total,), token = launch(
        middle_kernel, token, [index, *terms], [SMEM] + [VMEM] * len(terms),
        [VMEM], [array((NSUB * SUB, ROWS, GRID))], "add_middle", 4,
    )
    return total, token


def late_kernel(index, total, same, cross, out, fresh, sems):
    core = place()[2]
    base = index[ROUNDS] * SUB
    other = (NSUB - 1) * SUB - base
    copies = [(total.at[pl.ds(other, SUB)], out.at[pl.ds(other, SUB)])]
    copies += [
        (total.at[pl.ds(base + HALF * k, 1)], out.at[pl.ds(base + HALF * k, 1)]) for k in range(CORES)
    ]
    started = [pltpu.make_async_copy(*copy, sems.at[k]) for k, copy in enumerate(copies)]
    for copy in started:
        copy.start()
    for k, (part, target) in enumerate(((same, core), (cross, 1 - core))):
        band = base + target * HALF + 1
        fresh[k] = total[band] + part[0, 0]
        copy = pltpu.make_async_copy(
            fresh.at[pl.ds(k, 1)], out.at[pl.ds(band, 1)], sems.at[len(started)]
        )
        copy.start()
        started.append(copy)
    for copy in started:
        copy.wait()


def add_late(token, index, total, terms):
    (total,), token = launch(
        late_kernel, token, [index, total, *terms], [SMEM] + [VMEM] * 3, [HBM],
        [array(total.shape)], "add_late", 4,
        scratch=[pltpu.VMEM((CORES, ROWS, GRID), F32), pltpu.SemaphoreType.DMA((1 + 2 * CORES,))],
    )
    return total


def body(orbitals, plan):
    bands = lax.axis_size("band")
    spots = lax.axis_size("grid")

    def move(value, target):
        pairs = []
        for band in range(bands):
            for spot in range(spots):
                z, y, core = spot // (YS * CORES), (spot // CORES) % YS, spot % CORES
                b2, z2, y2, c2 = target(band, z, y, core)
                pairs.append((band * spots + spot, (b2 % bands) * spots + (z2 * YS + y2 % YS) * CORES + c2))
        return lax.ppermute(value, ("band", "grid"), pairs)

    def swap_cores(value):
        return move(value, lambda b, z, y, c: (b, z, y, 1 - c))

    def shift(value, steps):
        return move(value, lambda b, z, y, c: (b + steps, z, y, c))

    def there_and_across(values, steps):
        return [shift(values[0], steps), move(values[1], lambda b, z, y, c: (b + steps, z, y, 1 - c))]

    def along_y(messages, sign):
        return [messages[0]] + [
            move(messages[k], lambda b, z, y, c, k=k: (b, z, y + YS + sign * k, c)) for k in range(1, YS)
        ]

    chips, runs = tables()[5:7]
    blocks = orbitals.reshape(NSUB * SUB, PLANES, GRID, GRID).transpose(0, 2, 1, 3)
    blocks = blocks.reshape(NSUB * SUB, ROWS, GRID)
    both = (blocks, swap_cores(blocks))
    index, *sends, token = pick(plan, both)
    parts = [shift(sends[0], 1), shift(sends[1], -2)]
    own, token = pick_own(token, index, both)
    chains = [{} for _ in CHAINS]

    def start(at):
        nonlocal token
        step, members = CHAINS[at]
        chain = chains[at]
        chain["spec"], sums, token = forward(token, step, members, own, parts[step])
        chain["sums"] = along_y(sums, 1)

    def run(at, after=()):
        nonlocal token
        chain = chains[at]
        (chain["run"],), token = small(run_kernel, token, [*chain["sums"], chips], 1, "run", after=after)
        chain["near"] = move(chain["run"], lambda b, z, y, c: (b, z ^ 1, y, c))

    def two(at):
        nonlocal token
        chain = chains[at]
        (chain["two"],), token = small(two_kernel, token, [chain["run"], chain["near"], runs], 1, "two")
        chain["far"] = move(chain["two"], lambda b, z, y, c: (b, z ^ 2, y, c))

    def edges(at, after=()):
        nonlocal token
        chain = chains[at]
        args = [*chain["sums"], chain["near"], chain["two"], chain["far"], chips, runs]
        outs, token = small(
            edges_kernel, token, args, YS, "edges", [pltpu.VMEM((YS, *chain["run"].shape), F32)], after
        )
        chain["edges"] = along_y(outs, -1)

    def finish(at, prior=(), extra=(), after=()):
        nonlocal token
        step, members = CHAINS[at]
        chain = chains[at]
        terms, sums, token = backward(
            token, step, members, chain["spec"], chain["edges"], own, parts[step], prior, extra, after
        )
        return terms, sums

    second, first, last = range(len(CHAINS))
    start(second)
    run(second)
    start(first)
    start(last)
    run(first, [chains[second]["near"]])
    two(first)
    two(second)
    run(last)
    edges(first)
    two(last)
    terms_a, sums_a = finish(first, after=[chains[last]["far"]])
    back_a = shift(terms_a, -1)
    edges(last)
    edges(second)
    terms_b, sums_b = finish(second)
    terms_a, sums_a = finish(last, sums_a, sums_b[1:])
    final = there_and_across((terms_a[:1], terms_a[1:]), -1)
    back_b = there_and_across((terms_b[:1], terms_b[1:]), 2)
    total, token = add_early(token, index, [sums_a[0], sums_b[0]])
    total, token = add_middle(
        token, index, [total, swap_cores(sums_a[1]), *back_b, back_a, swap_cores(back_a[1:])]
    )
    total = add_late(token, index, total, final)
    total = total.reshape(NSUB * SUB, GRID, PLANES, GRID).transpose(0, 2, 1, 3)
    return total.reshape(NSUB * SUB, PLANES, GRID * GRID)


def solution(mesh):
    in_specs = (P("band", "grid", None), P())
    out_specs = P("band", "grid", None)
    return jax.shard_map(body, mesh=mesh, in_specs=in_specs, out_specs=out_specs, check_vma=False)
```

```python
import functools
import math

import jax
import jax.numpy as jnp
import ml_dtypes
import numpy as np
from jax import lax
from jax.experimental import pallas as pl
from jax.experimental.pallas import tpu as pltpu
from jax.sharding import PartitionSpec as P

GRID = 128
SUB = 4
NSUB = 2
ROUNDS = 2
CORES = 2
YS = 4
ZS = 4
PLANES = 4
ROWS = GRID * PLANES
HALF = SUB // CORES
QUARTER = GRID // YS
EDGE = 2 * QUARTER
CHAINS = ((1, (0, 1)), (0, (0,)), (0, (1,)))
F32 = jnp.float32
BF16 = jnp.bfloat16


@functools.cache
def tables():
    index = np.arange(GRID, dtype=np.int64)
    angle = (index[:, None] * index[None, :] % GRID) * (2.0 * math.pi / GRID)
    cas = (np.cos(angle) + np.sin(angle)).astype(np.float32)
    high = cas.astype(ml_dtypes.bfloat16)
    low = (cas - high.astype(np.float32)).astype(ml_dtypes.bfloat16)
    zero = np.zeros_like(high)
    right = np.block([[high, low], [high, zero]])
    left = np.block([[high, high], [low, zero]])
    roots = 2.0 - 2.0 * np.cos(index * (2.0 * math.pi / GRID))
    screen = (4.0 * math.pi / GRID) ** 2
    shift = screen + roots[:, None] + roots[None, :]
    spread = np.sqrt(shift + shift * shift / 4.0)
    decay = 1.0 / (1.0 + shift / 2.0 + spread)
    scale = 1.0 / (2.0 * spread * GRID**2)
    mean = np.zeros((1, GRID))
    mean[0, 0] = 2.0 * spread[0, 0] / (GRID * screen)
    chips = np.stack([decay ** (8 * k) for k in range(YS)])
    runs = np.stack([decay**32, decay**64, 1.0 / (1.0 - decay**GRID)])
    as32 = lambda value: np.asarray(value, dtype=np.float32)
    return right, left, as32(decay), as32(scale), as32(mean), as32(chips), as32(runs)


def split(value):
    high = value.astype(BF16)
    low = (value - high.astype(F32)).astype(BF16)
    return high, low


def times_right(value, table):
    full = jnp.dot(jnp.concatenate(split(value), axis=1), table, preferred_element_type=F32)
    return full[:, :GRID] + full[:, GRID:]


def times_left(value, table):
    full = jnp.dot(table, jnp.concatenate(split(value), axis=0), preferred_element_type=F32)
    return full[:GRID] + full[GRID:]


def place():
    spot = lax.axis_index("grid")
    return spot // (YS * CORES), (spot // CORES) % YS, spot % CORES


def quarter_of(which):
    return pl.ds(pl.multiple_of(which * QUARTER, QUARTER), QUARTER)


def array(shape, dtype=F32):
    return jax.ShapeDtypeStruct(tuple(shape), dtype)


HBM = pl.BlockSpec(memory_space=pltpu.HBM)
VMEM = pl.BlockSpec(memory_space=pltpu.VMEM)
SMEM = pl.BlockSpec(memory_space=pltpu.SMEM)


def launch(kernel, token, args, in_specs, out_specs, out_shape, name, limit, grid=(), scratch=(), after=(), work=0):
    tokens = [] if token is None else [token]
    ins, outs, waits = len(args), len(out_shape), len(tokens) + len(after)
    unread = pl.BlockSpec(memory_space=pl.ANY)

    def ordered(*refs):
        kernel(*refs[:ins], *refs[ins + waits : ins + waits + outs], *refs[ins + waits + outs + 1 :])

    result = pl.pallas_call(
        ordered,
        grid=grid,
        in_specs=[*in_specs, *[unread] * waits],
        out_specs=[*out_specs, unread],
        scratch_shapes=list(scratch),
        out_shape=[*out_shape, array((8, GRID))],
        compiler_params=pltpu.CompilerParams(vmem_limit_bytes=limit << 20),
        cost_estimate=pl.CostEstimate(flops=work, bytes_accessed=work // 256, transcendentals=0),
        name=name,
    )(*args, *tokens, *after)
    return result[:-1], result[-1]


def message(pairs):
    return array((pairs * EDGE + 8, GRID))


def pairs_of(ref):
    return ref.shape[0] // EDGE


def copy_all(copies, sems):
    started = []
    for number, (source, target) in enumerate(copies):
        copy = pltpu.make_async_copy(source, target, sems.at[number])
        copy.start()
        started.append(copy)
    for copy in started:
        copy.wait()


def pick_kernel(plan, own_a, own_b, index, first, second, sems):
    band_count = lax.axis_size("band")
    band_me = lax.axis_index("band")
    core = place()[2]
    index[0] = plan[0, band_me, 0]
    index[1] = plan[1, (band_me + 2) % band_count, 1]
    index[2] = plan[0, (band_me + 1) % band_count, 1]
    index[3] = plan[1, band_me, 0]
    copies = []
    for step, out in enumerate((first, second)):
        start = index[ROUNDS + step] * SUB + core * HALF
        for source, own in enumerate((own_a, own_b)):
            copies.append((own.at[pl.ds(start, HALF)], out.at[source]))
    copy_all(copies, sems)


def pick(plan, own):
    two = array((CORES, HALF, ROWS, GRID))
    outs, token = launch(
        pick_kernel, None, [plan, *own], [SMEM, HBM, VMEM], [SMEM] + [VMEM] * 2,
        [array((2 * ROUNDS,), jnp.int32), two, two], "pick", 2,
        scratch=[pltpu.SemaphoreType.DMA((2 * CORES,))],
    )
    return *outs, token


def pick_own_kernel(index, own_a, own_b, out, sems):
    copy_all(
        [
            (own.at[pl.ds(index[step] * SUB, SUB)], out.at[step, source])
            for step in range(ROUNDS)
            for source, own in enumerate((own_a, own_b))
        ],
        sems,
    )


def pick_own(token, index, own):
    (out,), token = launch(
        pick_own_kernel, token, [index, *own], [SMEM, HBM, VMEM], [VMEM],
        [array((ROUNDS, CORES, SUB, ROWS, GRID))], "pick_own", 2,
        scratch=[pltpu.SemaphoreType.DMA((ROUNDS * CORES,))],
    )
    return out, token


def forward_kernel(step, member, own, part, right, left, decay, scale, spec, a, b, c, d, lines):
    outs = (a, b, c, d)
    _, y, core = place()
    j = pl.program_id(0)
    for i in range(SUB):
        for source in range(CORES):
            spot = i * CORES + source
            lines[spot] = times_right(own[step, source, i] * part[source, member + j], right[...])
            half = (core if source == 0 else 1 - core) * PLANES
            for x in range(0, PLANES, 2):
                two = jnp.concatenate(
                    [lines[spot, pl.ds(x + k, GRID, stride=PLANES), :] for k in range(2)], axis=1
                )
                two = times_left(two, left[...])
                for k in range(2):
                    spec[j * SUB + i, half + x + k] = two[:, k * GRID : (k + 1) * GRID] * scale[...]
    for i in range(SUB):
        pair = j * SUB + i
        base = pl.multiple_of(pair * EDGE, EDGE)
        total = spec[pair, 0, 0:1, :]
        for x in range(1, 2 * PLANES):
            total = total + spec[pair, x, 0:1, :]
        for k in range(YS):
            rows = quarter_of((y + k) % YS)
            ratio = decay[rows, :]
            planes = [spec[pair, x, rows, :] for x in range(2 * PLANES)]
            ahead, behind = planes[0], planes[-1]
            for x in range(1, 2 * PLANES):
                ahead = planes[x] + ratio * ahead
                behind = planes[-1 - x] + ratio * behind
            outs[k][pl.ds(base, QUARTER), :] = ahead
            outs[k][pl.ds(base + QUARTER, QUARTER), :] = behind
            outs[k][pl.ds(pairs_of(a) * EDGE + pair, 1), :] = total


def forward(token, step, members, own, part):
    right, left, decay, scale = tables()[:4]
    pairs = len(members) * SUB
    outs, token = launch(
        functools.partial(forward_kernel, step, members[0]),
        token,
        [own, part, right, left, decay, scale],
        [VMEM] * 6,
        [VMEM] * (1 + YS),
        [array((pairs, 2 * PLANES, GRID, GRID))] + [message(pairs)] * YS,
        "forward", 12, grid=(len(members),),
        scratch=[pltpu.VMEM((SUB * CORES, ROWS, GRID), F32)],
    )
    return outs[0], outs[1:], token


def run_kernel(a, b, c, d, chips, out):
    _, y, _ = place()
    rows = quarter_of(y)
    got = (a, b, c, d)
    from_chip = [(y - k + YS) % YS for k in range(YS)]
    ahead = [chips[YS - 1 - chip, rows, :] for chip in from_chip]
    behind = [chips[chip, rows, :] for chip in from_chip]
    for pair in range(pairs_of(out)):
        base = pair * EDGE
        for weights, start in ((ahead, base), (behind, base + QUARTER)):
            at = slice(start, start + QUARTER)
            out[at, :] = sum(got[k][at, :] * weights[k] for k in range(YS))
    at = slice(pairs_of(out) * EDGE, pairs_of(out) * EDGE + 8)
    out[at, :] = sum(got[k][at, :] for k in range(YS))


def two_kernel(mine, other, runs, out):
    z, y, _ = place()
    power = runs[0, quarter_of(y), :]
    odd = (jnp.zeros(power.shape, jnp.int32) + z % 2) == 1
    ones = jnp.ones_like(power)
    first = jnp.where(odd, ones, power)
    second = jnp.where(odd, power, ones)
    for pair in range(pairs_of(out)):
        base = pair * EDGE
        at = slice(base, base + QUARTER)
        out[at, :] = mine[at, :] * first + other[at, :] * second
        at = slice(base + QUARTER, base + 2 * QUARTER)
        out[at, :] = mine[at, :] * second + other[at, :] * first
    at = slice(pairs_of(mine) * EDGE, pairs_of(mine) * EDGE + 8)
    out[at, :] = mine[at, :] + other[at, :]


def edges_kernel(a, b, c, d, near, mine, other, chips, runs, *rest):
    outs, held = rest[:YS], rest[YS]
    z, y, _ = place()
    rows = quarter_of(y)
    got = (a, b, c, d)
    step, run, two, wrap = chips[1, rows, :], runs[0, rows, :], runs[1, rows, :], runs[2, rows, :]
    odd = (jnp.zeros(step.shape, jnp.int32) + z % 2) == 1
    for k in range(YS):
        held[(y - k + YS) % YS] = got[k][...]
    for pair in range(pairs_of(a)):
        base = pair * EDGE
        ahead = slice(base, base + QUARTER)
        behind = slice(base + QUARTER, base + 2 * QUARTER)
        from_left = (other[ahead, :] + two * mine[ahead, :]) * wrap
        from_right = (other[behind, :] + two * mine[behind, :]) * wrap
        from_left = jnp.where(odd, near[ahead, :] + run * from_left, from_left)
        from_right = jnp.where(odd, from_right, near[behind, :] + run * from_right)
        for chip in range(YS):
            chip_ahead = held[chip, ahead, :]
            held[chip, ahead, :] = from_left
            from_left = chip_ahead + step * from_left
        for chip in reversed(range(YS)):
            chip_behind = held[chip, behind, :]
            held[chip, behind, :] = from_right
            from_right = chip_behind + step * from_right
    at = slice(pairs_of(mine) * EDGE, pairs_of(mine) * EDGE + 8)
    total = mine[at, :] + other[at, :]
    for k in range(YS):
        outs[k][...] = held[(y - k + YS) % YS]
        outs[k][at, :] = total


def small(kernel, token, args, count, name, scratch=(), after=()):
    return launch(
        kernel, token, args, [VMEM] * len(args), [VMEM] * count, [array(args[0].shape)] * count, name, 6,
        scratch=scratch, after=after,
    )


def backward_kernel(step, member, prior, extra, spec, a, b, c, d, own, part, right, left, decay, mean, *rest):
    before, (part_out, own_out_a, own_out_b, field, lines) = rest[: prior + extra], rest[prior + extra :]
    j = pl.program_id(0)
    edges = (a, b, c, d)
    _, y, core = place()
    for i in range(SUB):
        pair = j * SUB + i
        base = pl.multiple_of(pair * EDGE, EDGE)
        for k in range(YS):
            rows = quarter_of((y + k) % YS)
            ratio = decay[rows, :]
            planes = [spec[pair, x, rows, :] for x in range(2 * PLANES)]
            ahead = edges[k][pl.ds(base, QUARTER), :]
            behind = edges[k][pl.ds(base + QUARTER, QUARTER), :]
            sums = []
            for x in range(2 * PLANES):
                ahead = planes[x] + ratio * ahead
                sums.append(ahead)
            for x in reversed(range(2 * PLANES)):
                behind = ratio * behind
                field[i, x, rows, :] = sums[x] + behind
                behind = planes[x] + behind
        average = a[pl.ds(pairs_of(a) * EDGE + pair, 1), :] * mean[...]
        for x in range(2 * PLANES):
            field[i, x, 0:1, :] = field[i, x, 0:1, :] - average
    for source, own_out in enumerate((own_out_a, own_out_b)):
        half = (core if source == 0 else 1 - core) * PLANES
        added = None
        for i in range(SUB):
            spot = i * CORES + source
            for x in range(0, PLANES, 2):
                two = jnp.concatenate([field[i, half + x + k] for k in range(2)], axis=1)
                two = times_left(two, left[...])
                for k in range(2):
                    lines[spot, pl.ds(x + k, GRID, stride=PLANES), :] = two[:, k * GRID : (k + 1) * GRID]
            potential = times_right(lines[spot], right[...])
            to_part = potential * own[step, source, i]
            to_own = potential * part[source, member + j]
            added = to_part if added is None else added + to_part
            if prior:
                own_out[i] = before[source][i] - to_own
            else:
                own_out[i] = jnp.where(j == 0, 0.0, own_out[i]) - to_own
        part_out[source, j] = -added
    if extra:
        own_out_b[SUB : 2 * SUB] = before[prior][...]


def backward(token, step, members, spec, edges, own, part, prior=(), extra=(), after=()):
    right, left, decay, _, mean = tables()[:5]
    args = [spec, *edges, own, part, right, left, decay, mean, *prior, *extra]
    outs, token = launch(
        functools.partial(backward_kernel, step, members[0], len(prior), len(extra)),
        token,
        args,
        [VMEM] * len(args),
        [VMEM] * 3,
        [
            array((CORES, len(members), ROWS, GRID)),
            array((SUB, ROWS, GRID)),
            array((2 * SUB if extra else SUB, ROWS, GRID)),
        ],
        "backward", 12, grid=(len(members),),
        scratch=[
            pltpu.VMEM((SUB, 2 * PLANES, GRID, GRID), F32),
            pltpu.VMEM((SUB * CORES, ROWS, GRID), F32),
        ],
        after=after,
    )
    return outs[0], outs[1:], token


def early_kernel(index, own_first, own_second, out):
    for i in range(SUB):
        out[index[0] * SUB + i] = own_first[i]
        out[(NSUB - 1 - index[0]) * SUB + i] = jnp.zeros((ROWS, GRID), F32)
    for i in range(SUB):
        band = index[1] * SUB + i
        out[band] = out[band] + own_second[i]


def add_early(token, index, terms):
    (total,), token = launch(
        early_kernel, token, [index, *terms], [SMEM] + [VMEM] * len(terms),
        [VMEM], [array((NSUB * SUB, ROWS, GRID))], "add_early", 4, work=40_000_000_000,
    )
    return total, token


def middle_kernel(index, total, swapped, same, cross, first_same, first_cross, out):
    core = place()[2]
    for band in range(NSUB * SUB):
        out[band] = total[band]
    for step in range(ROUNDS):
        for i in range(SUB):
            band = index[step] * SUB + i
            out[band] = out[band] + swapped[step * SUB + i]
    for part, target in ((same, core), (cross, 1 - core)):
        for member in range(HALF):
            band = index[ROUNDS + 1] * SUB + target * HALF + member
            out[band] = out[band] + part[0, member]
    for part, target in ((first_same, core), (first_cross, 1 - core)):
        band = index[ROUNDS] * SUB + target * HALF
        out[band] = out[band] + part[0, 0]


def add_middle(token, index, terms):
    (total,), token = launch(
        middle_kernel, token, [index, *terms], [SMEM] + [VMEM] * len(terms),
        [VMEM], [array((NSUB * SUB, ROWS, GRID))], "add_middle", 4,
    )
    return total, token


def late_kernel(index, total, same, cross, out, fresh, sems):
    core = place()[2]
    base = index[ROUNDS] * SUB
    other = (NSUB - 1) * SUB - base
    copies = [(total.at[pl.ds(other, SUB)], out.at[pl.ds(other, SUB)])]
    copies += [
        (total.at[pl.ds(base + HALF * k, 1)], out.at[pl.ds(base + HALF * k, 1)]) for k in range(CORES)
    ]
    started = [pltpu.make_async_copy(*copy, sems.at[k]) for k, copy in enumerate(copies)]
    for copy in started:
        copy.start()
    for k, (part, target) in enumerate(((same, core), (cross, 1 - core))):
        band = base + target * HALF + 1
        fresh[k] = total[band] + part[0, 0]
        copy = pltpu.make_async_copy(
            fresh.at[pl.ds(k, 1)], out.at[pl.ds(band, 1)], sems.at[len(started)]
        )
        copy.start()
        started.append(copy)
    for copy in started:
        copy.wait()


def add_late(token, index, total, terms):
    (total,), token = launch(
        late_kernel, token, [index, total, *terms], [SMEM] + [VMEM] * 3, [HBM],
        [array(total.shape)], "add_late", 4,
        scratch=[pltpu.VMEM((CORES, ROWS, GRID), F32), pltpu.SemaphoreType.DMA((1 + 2 * CORES,))],
    )
    return total


def body(orbitals, plan):
    bands = lax.axis_size("band")
    spots = lax.axis_size("grid")

    def move(value, target):
        pairs = []
        for band in range(bands):
            for spot in range(spots):
                z, y, core = spot // (YS * CORES), (spot // CORES) % YS, spot % CORES
                b2, z2, y2, c2 = target(band, z, y, core)
                pairs.append((band * spots + spot, (b2 % bands) * spots + (z2 * YS + y2 % YS) * CORES + c2))
        return lax.ppermute(value, ("band", "grid"), pairs)

    def swap_cores(value):
        return move(value, lambda b, z, y, c: (b, z, y, 1 - c))

    def shift(value, steps):
        return move(value, lambda b, z, y, c: (b + steps, z, y, c))

    def there_and_across(values, steps):
        return [shift(values[0], steps), move(values[1], lambda b, z, y, c: (b + steps, z, y, 1 - c))]

    def along_y(messages, sign):
        return [messages[0]] + [
            move(messages[k], lambda b, z, y, c, k=k: (b, z, y + YS + sign * k, c)) for k in range(1, YS)
        ]

    chips, runs = tables()[5:7]
    blocks = orbitals.reshape(NSUB * SUB, PLANES, GRID, GRID).transpose(0, 2, 1, 3)
    blocks = blocks.reshape(NSUB * SUB, ROWS, GRID)
    both = (blocks, swap_cores(blocks))
    index, *sends, token = pick(plan, both)
    parts = [shift(sends[0], 1), shift(sends[1], -2)]
    own, token = pick_own(token, index, both)
    chains = [{} for _ in CHAINS]

    def start(at):
        nonlocal token
        step, members = CHAINS[at]
        chain = chains[at]
        chain["spec"], sums, token = forward(token, step, members, own, parts[step])
        chain["sums"] = along_y(sums, 1)

    def run(at, after=()):
        nonlocal token
        chain = chains[at]
        (chain["run"],), token = small(run_kernel, token, [*chain["sums"], chips], 1, "run", after=after)
        chain["near"] = move(chain["run"], lambda b, z, y, c: (b, z ^ 1, y, c))

    def two(at):
        nonlocal token
        chain = chains[at]
        (chain["two"],), token = small(two_kernel, token, [chain["run"], chain["near"], runs], 1, "two")
        chain["far"] = move(chain["two"], lambda b, z, y, c: (b, z ^ 2, y, c))

    def edges(at, after=()):
        nonlocal token
        chain = chains[at]
        args = [*chain["sums"], chain["near"], chain["two"], chain["far"], chips, runs]
        outs, token = small(
            edges_kernel, token, args, YS, "edges", [pltpu.VMEM((YS, *chain["run"].shape), F32)], after
        )
        chain["edges"] = along_y(outs, -1)

    def finish(at, prior=(), extra=(), after=()):
        nonlocal token
        step, members = CHAINS[at]
        chain = chains[at]
        terms, sums, token = backward(
            token, step, members, chain["spec"], chain["edges"], own, parts[step], prior, extra, after
        )
        return terms, sums

    second, first, last = range(len(CHAINS))
    start(second)
    run(second)
    start(first)
    start(last)
    run(first, [chains[second]["near"]])
    two(first)
    two(second)
    run(last)
    edges(first)
    two(last)
    edges(second)
    terms_a, sums_a = finish(first, after=[chains[last]["far"]])
    back_a = shift(terms_a, -1)
    edges(last)
    terms_b, sums_b = finish(second)
    terms_a, sums_a = finish(last, sums_a, sums_b[1:])
    final = there_and_across((terms_a[:1], terms_a[1:]), -1)
    back_b = there_and_across((terms_b[:1], terms_b[1:]), 2)
    total, token = add_early(token, index, [sums_a[0], sums_b[0]])
    total, token = add_middle(
        token, index, [total, swap_cores(sums_a[1]), *back_b, back_a, swap_cores(back_a[1:])]
    )
    total = add_late(token, index, total, final)
    total = total.reshape(NSUB * SUB, GRID, PLANES, GRID).transpose(0, 2, 1, 3)
    return total.reshape(NSUB * SUB, PLANES, GRID * GRID)


def solution(mesh):
    in_specs = (P("band", "grid", None), P())
    out_specs = P("band", "grid", None)
    return jax.shard_map(body, mesh=mesh, in_specs=in_specs, out_specs=out_specs, check_vma=False)
```

```python
import functools
import math

import jax
import jax.numpy as jnp
import ml_dtypes
import numpy as np
from jax import lax
from jax.experimental import pallas as pl
from jax.experimental.pallas import tpu as pltpu
from jax.sharding import PartitionSpec as P

GRID = 128
SUB = 4
NSUB = 2
ROUNDS = 2
CORES = 2
YS = 4
ZS = 4
PLANES = 4
ROWS = GRID * PLANES
HALF = SUB // CORES
QUARTER = GRID // YS
EDGE = 2 * QUARTER
CHAINS = ((1, (0, 1)), (0, (0,)), (0, (1,)))
F32 = jnp.float32
BF16 = jnp.bfloat16


@functools.cache
def tables():
    index = np.arange(GRID, dtype=np.int64)
    angle = (index[:, None] * index[None, :] % GRID) * (2.0 * math.pi / GRID)
    cas = (np.cos(angle) + np.sin(angle)).astype(np.float32)
    high = cas.astype(ml_dtypes.bfloat16)
    low = (cas - high.astype(np.float32)).astype(ml_dtypes.bfloat16)
    zero = np.zeros_like(high)
    right = np.block([[high, low], [high, zero]])
    left = np.block([[high, high], [low, zero]])
    roots = 2.0 - 2.0 * np.cos(index * (2.0 * math.pi / GRID))
    screen = (4.0 * math.pi / GRID) ** 2
    shift = screen + roots[:, None] + roots[None, :]
    spread = np.sqrt(shift + shift * shift / 4.0)
    decay = 1.0 / (1.0 + shift / 2.0 + spread)
    scale = 1.0 / (2.0 * spread * GRID**2)
    mean = np.zeros((1, GRID))
    mean[0, 0] = 2.0 * spread[0, 0] / (GRID * screen)
    chips = np.stack([decay ** (8 * k) for k in range(YS)])
    runs = np.stack([decay**32, decay**64, 1.0 / (1.0 - decay**GRID)])
    as32 = lambda value: np.asarray(value, dtype=np.float32)
    return right, left, as32(decay), as32(scale), as32(mean), as32(chips), as32(runs)


def split(value):
    high = value.astype(BF16)
    low = (value - high.astype(F32)).astype(BF16)
    return high, low


def times_right(value, table):
    full = jnp.dot(jnp.concatenate(split(value), axis=1), table, preferred_element_type=F32)
    return full[:, :GRID] + full[:, GRID:]


def times_left(value, table):
    full = jnp.dot(table, jnp.concatenate(split(value), axis=0), preferred_element_type=F32)
    return full[:GRID] + full[GRID:]


def place():
    spot = lax.axis_index("grid")
    return spot // (YS * CORES), (spot // CORES) % YS, spot % CORES


def quarter_of(which):
    return pl.ds(pl.multiple_of(which * QUARTER, QUARTER), QUARTER)


def array(shape, dtype=F32):
    return jax.ShapeDtypeStruct(tuple(shape), dtype)


HBM = pl.BlockSpec(memory_space=pltpu.HBM)
VMEM = pl.BlockSpec(memory_space=pltpu.VMEM)
SMEM = pl.BlockSpec(memory_space=pltpu.SMEM)


def launch(kernel, token, args, in_specs, out_specs, out_shape, name, limit, grid=(), scratch=(), after=(), work=0):
    tokens = [] if token is None else [token]
    ins, outs, waits = len(args), len(out_shape), len(tokens) + len(after)
    unread = pl.BlockSpec(memory_space=pl.ANY)

    def ordered(*refs):
        kernel(*refs[:ins], *refs[ins + waits : ins + waits + outs], *refs[ins + waits + outs + 1 :])

    result = pl.pallas_call(
        ordered,
        grid=grid,
        in_specs=[*in_specs, *[unread] * waits],
        out_specs=[*out_specs, unread],
        scratch_shapes=list(scratch),
        out_shape=[*out_shape, array((8, GRID))],
        compiler_params=pltpu.CompilerParams(vmem_limit_bytes=limit << 20),
        cost_estimate=pl.CostEstimate(flops=work, bytes_accessed=work // 256, transcendentals=0),
        name=name,
    )(*args, *tokens, *after)
    return result[:-1], result[-1]


def message(pairs):
    return array((pairs * EDGE + 8, GRID))


def pairs_of(ref):
    return ref.shape[0] // EDGE


def copy_all(copies, sems):
    started = []
    for number, (source, target) in enumerate(copies):
        copy = pltpu.make_async_copy(source, target, sems.at[number])
        copy.start()
        started.append(copy)
    for copy in started:
        copy.wait()


def pick_kernel(plan, own_a, own_b, index, first, second, sems):
    band_count = lax.axis_size("band")
    band_me = lax.axis_index("band")
    core = place()[2]
    index[0] = plan[0, band_me, 0]
    index[1] = plan[1, (band_me + 2) % band_count, 1]
    index[2] = plan[0, (band_me + 1) % band_count, 1]
    index[3] = plan[1, band_me, 0]
    copies = []
    for step, out in enumerate((first, second)):
        start = index[ROUNDS + step] * SUB + core * HALF
        for source, own in enumerate((own_a, own_b)):
            copies.append((own.at[pl.ds(start, HALF)], out.at[source]))
    copy_all(copies, sems)


def pick(plan, own):
    two = array((CORES, HALF, ROWS, GRID))
    outs, token = launch(
        pick_kernel, None, [plan, *own], [SMEM, HBM, VMEM], [SMEM] + [VMEM] * 2,
        [array((2 * ROUNDS,), jnp.int32), two, two], "pick", 2,
        scratch=[pltpu.SemaphoreType.DMA((2 * CORES,))],
    )
    return *outs, token


def pick_own_kernel(index, own_a, own_b, out, sems):
    copy_all(
        [
            (own.at[pl.ds(index[step] * SUB, SUB)], out.at[step, source])
            for step in range(ROUNDS)
            for source, own in enumerate((own_a, own_b))
        ],
        sems,
    )


def pick_own(token, index, own):
    (out,), token = launch(
        pick_own_kernel, token, [index, *own], [SMEM, HBM, VMEM], [VMEM],
        [array((ROUNDS, CORES, SUB, ROWS, GRID))], "pick_own", 2,
        scratch=[pltpu.SemaphoreType.DMA((ROUNDS * CORES,))],
    )
    return out, token


def forward_kernel(step, member, own, part, right, left, decay, scale, spec, a, b, c, d, lines):
    outs = (a, b, c, d)
    _, y, core = place()
    j = pl.program_id(0)
    for i in range(SUB):
        for source in range(CORES):
            spot = i * CORES + source
            lines[spot] = times_right(own[step, source, i] * part[source, member + j], right[...])
            half = (core if source == 0 else 1 - core) * PLANES
            for x in range(0, PLANES, 2):
                two = jnp.concatenate(
                    [lines[spot, pl.ds(x + k, GRID, stride=PLANES), :] for k in range(2)], axis=1
                )
                two = times_left(two, left[...])
                for k in range(2):
                    spec[j * SUB + i, half + x + k] = two[:, k * GRID : (k + 1) * GRID] * scale[...]
    for i in range(SUB):
        pair = j * SUB + i
        base = pl.multiple_of(pair * EDGE, EDGE)
        total = spec[pair, 0, 0:1, :]
        for x in range(1, 2 * PLANES):
            total = total + spec[pair, x, 0:1, :]
        for k in range(YS):
            rows = quarter_of((y + k) % YS)
            ratio = decay[rows, :]
            planes = [spec[pair, x, rows, :] for x in range(2 * PLANES)]
            ahead, behind = planes[0], planes[-1]
            for x in range(1, 2 * PLANES):
                ahead = planes[x] + ratio * ahead
                behind = planes[-1 - x] + ratio * behind
            outs[k][pl.ds(base, QUARTER), :] = ahead
            outs[k][pl.ds(base + QUARTER, QUARTER), :] = behind
            outs[k][pl.ds(pairs_of(a) * EDGE + pair, 1), :] = total


def forward(token, step, members, own, part):
    right, left, decay, scale = tables()[:4]
    pairs = len(members) * SUB
    outs, token = launch(
        functools.partial(forward_kernel, step, members[0]),
        token,
        [own, part, right, left, decay, scale],
        [VMEM] * 6,
        [VMEM] * (1 + YS),
        [array((pairs, 2 * PLANES, GRID, GRID))] + [message(pairs)] * YS,
        "forward", 12, grid=(len(members),),
        scratch=[pltpu.VMEM((SUB * CORES, ROWS, GRID), F32)],
    )
    return outs[0], outs[1:], token


def run_kernel(a, b, c, d, chips, out):
    _, y, _ = place()
    rows = quarter_of(y)
    got = (a, b, c, d)
    from_chip = [(y - k + YS) % YS for k in range(YS)]
    ahead = [chips[YS - 1 - chip, rows, :] for chip in from_chip]
    behind = [chips[chip, rows, :] for chip in from_chip]
    for pair in range(pairs_of(out)):
        base = pair * EDGE
        for weights, start in ((ahead, base), (behind, base + QUARTER)):
            at = slice(start, start + QUARTER)
            out[at, :] = sum(got[k][at, :] * weights[k] for k in range(YS))
    at = slice(pairs_of(out) * EDGE, pairs_of(out) * EDGE + 8)
    out[at, :] = sum(got[k][at, :] for k in range(YS))


def two_kernel(mine, other, runs, out):
    z, y, _ = place()
    power = runs[0, quarter_of(y), :]
    odd = (jnp.zeros(power.shape, jnp.int32) + z % 2) == 1
    ones = jnp.ones_like(power)
    first = jnp.where(odd, ones, power)
    second = jnp.where(odd, power, ones)
    for pair in range(pairs_of(out)):
        base = pair * EDGE
        at = slice(base, base + QUARTER)
        out[at, :] = mine[at, :] * first + other[at, :] * second
        at = slice(base + QUARTER, base + 2 * QUARTER)
        out[at, :] = mine[at, :] * second + other[at, :] * first
    at = slice(pairs_of(mine) * EDGE, pairs_of(mine) * EDGE + 8)
    out[at, :] = mine[at, :] + other[at, :]


def edges_kernel(a, b, c, d, near, mine, other, chips, runs, *rest):
    outs, held = rest[:YS], rest[YS]
    z, y, _ = place()
    rows = quarter_of(y)
    got = (a, b, c, d)
    step, run, two, wrap = chips[1, rows, :], runs[0, rows, :], runs[1, rows, :], runs[2, rows, :]
    odd = (jnp.zeros(step.shape, jnp.int32) + z % 2) == 1
    for k in range(YS):
        held[(y - k + YS) % YS] = got[k][...]
    for pair in range(pairs_of(a)):
        base = pair * EDGE
        ahead = slice(base, base + QUARTER)
        behind = slice(base + QUARTER, base + 2 * QUARTER)
        from_left = (other[ahead, :] + two * mine[ahead, :]) * wrap
        from_right = (other[behind, :] + two * mine[behind, :]) * wrap
        from_left = jnp.where(odd, near[ahead, :] + run * from_left, from_left)
        from_right = jnp.where(odd, from_right, near[behind, :] + run * from_right)
        for chip in range(YS):
            chip_ahead = held[chip, ahead, :]
            held[chip, ahead, :] = from_left
            from_left = chip_ahead + step * from_left
        for chip in reversed(range(YS)):
            chip_behind = held[chip, behind, :]
            held[chip, behind, :] = from_right
            from_right = chip_behind + step * from_right
    at = slice(pairs_of(mine) * EDGE, pairs_of(mine) * EDGE + 8)
    total = mine[at, :] + other[at, :]
    for k in range(YS):
        outs[k][...] = held[(y - k + YS) % YS]
        outs[k][at, :] = total


def small(kernel, token, args, count, name, scratch=(), after=()):
    return launch(
        kernel, token, args, [VMEM] * len(args), [VMEM] * count, [array(args[0].shape)] * count, name, 6,
        scratch=scratch, after=after,
    )


def backward_kernel(step, member, prior, extra, spec, a, b, c, d, own, part, right, left, decay, mean, *rest):
    before, (part_out, own_out_a, own_out_b, field, lines) = rest[: prior + extra], rest[prior + extra :]
    j = pl.program_id(0)
    edges = (a, b, c, d)
    _, y, core = place()
    for i in range(SUB):
        pair = j * SUB + i
        base = pl.multiple_of(pair * EDGE, EDGE)
        for k in range(YS):
            rows = quarter_of((y + k) % YS)
            ratio = decay[rows, :]
            planes = [spec[pair, x, rows, :] for x in range(2 * PLANES)]
            ahead = edges[k][pl.ds(base, QUARTER), :]
            behind = edges[k][pl.ds(base + QUARTER, QUARTER), :]
            sums = []
            for x in range(2 * PLANES):
                ahead = planes[x] + ratio * ahead
                sums.append(ahead)
            for x in reversed(range(2 * PLANES)):
                behind = ratio * behind
                field[i, x, rows, :] = sums[x] + behind
                behind = planes[x] + behind
        average = a[pl.ds(pairs_of(a) * EDGE + pair, 1), :] * mean[...]
        for x in range(2 * PLANES):
            field[i, x, 0:1, :] = field[i, x, 0:1, :] - average
    for source, own_out in enumerate((own_out_a, own_out_b)):
        half = (core if source == 0 else 1 - core) * PLANES
        added = None
        for i in range(SUB):
            spot = i * CORES + source
            for x in range(0, PLANES, 2):
                two = jnp.concatenate([field[i, half + x + k] for k in range(2)], axis=1)
                two = times_left(two, left[...])
                for k in range(2):
                    lines[spot, pl.ds(x + k, GRID, stride=PLANES), :] = two[:, k * GRID : (k + 1) * GRID]
            potential = times_right(lines[spot], right[...])
            to_part = potential * own[step, source, i]
            to_own = potential * part[source, member + j]
            added = to_part if added is None else added + to_part
            if prior:
                own_out[i] = before[source][i] - to_own
            else:
                own_out[i] = jnp.where(j == 0, 0.0, own_out[i]) - to_own
        part_out[source, j] = -added
    if extra:
        own_out_b[SUB : 2 * SUB] = before[prior][...]


def backward(token, step, members, spec, edges, own, part, prior=(), extra=()):
    right, left, decay, _, mean = tables()[:5]
    args = [spec, *edges, own, part, right, left, decay, mean, *prior, *extra]
    outs, token = launch(
        functools.partial(backward_kernel, step, members[0], len(prior), len(extra)),
        token,
        args,
        [VMEM] * len(args),
        [VMEM] * 3,
        [
            array((CORES, len(members), ROWS, GRID)),
            array((SUB, ROWS, GRID)),
            array((2 * SUB if extra else SUB, ROWS, GRID)),
        ],
        "backward", 12, grid=(len(members),),
        scratch=[
            pltpu.VMEM((SUB, 2 * PLANES, GRID, GRID), F32),
            pltpu.VMEM((SUB * CORES, ROWS, GRID), F32),
        ],
    )
    return outs[0], outs[1:], token


def early_kernel(index, own_first, own_second, out):
    for i in range(SUB):
        out[index[0] * SUB + i] = own_first[i]
        out[(NSUB - 1 - index[0]) * SUB + i] = jnp.zeros((ROWS, GRID), F32)
    for i in range(SUB):
        band = index[1] * SUB + i
        out[band] = out[band] + own_second[i]


def add_early(token, index, terms):
    (total,), token = launch(
        early_kernel, token, [index, *terms], [SMEM] + [VMEM] * len(terms),
        [VMEM], [array((NSUB * SUB, ROWS, GRID))], "add_early", 4, work=40_000_000_000,
    )
    return total, token


def middle_kernel(index, total, swapped, same, cross, first_same, first_cross, out):
    core = place()[2]
    for band in range(NSUB * SUB):
        out[band] = total[band]
    for step in range(ROUNDS):
        for i in range(SUB):
            band = index[step] * SUB + i
            out[band] = out[band] + swapped[step * SUB + i]
    for part, target in ((same, core), (cross, 1 - core)):
        for member in range(HALF):
            band = index[ROUNDS + 1] * SUB + target * HALF + member
            out[band] = out[band] + part[0, member]
    for part, target in ((first_same, core), (first_cross, 1 - core)):
        band = index[ROUNDS] * SUB + target * HALF
        out[band] = out[band] + part[0, 0]


def add_middle(token, index, terms):
    (total,), token = launch(
        middle_kernel, token, [index, *terms], [SMEM] + [VMEM] * len(terms),
        [VMEM], [array((NSUB * SUB, ROWS, GRID))], "add_middle", 4,
    )
    return total, token


def late_kernel(index, total, same, cross, out, fresh, sems):
    core = place()[2]
    base = index[ROUNDS] * SUB
    other = (NSUB - 1) * SUB - base
    copies = [(total.at[pl.ds(other, SUB)], out.at[pl.ds(other, SUB)])]
    copies += [
        (total.at[pl.ds(base + HALF * k, 1)], out.at[pl.ds(base + HALF * k, 1)]) for k in range(CORES)
    ]
    started = [pltpu.make_async_copy(*copy, sems.at[k]) for k, copy in enumerate(copies)]
    for copy in started:
        copy.start()
    for k, (part, target) in enumerate(((same, core), (cross, 1 - core))):
        band = base + target * HALF + 1
        fresh[k] = total[band] + part[0, 0]
        copy = pltpu.make_async_copy(
            fresh.at[pl.ds(k, 1)], out.at[pl.ds(band, 1)], sems.at[len(started)]
        )
        copy.start()
        started.append(copy)
    for copy in started:
        copy.wait()


def add_late(token, index, total, terms):
    (total,), token = launch(
        late_kernel, token, [index, total, *terms], [SMEM] + [VMEM] * 3, [HBM],
        [array(total.shape)], "add_late", 4,
        scratch=[pltpu.VMEM((CORES, ROWS, GRID), F32), pltpu.SemaphoreType.DMA((1 + 2 * CORES,))],
    )
    return total


def body(orbitals, plan):
    bands = lax.axis_size("band")
    spots = lax.axis_size("grid")

    def move(value, target):
        pairs = []
        for band in range(bands):
            for spot in range(spots):
                z, y, core = spot // (YS * CORES), (spot // CORES) % YS, spot % CORES
                b2, z2, y2, c2 = target(band, z, y, core)
                pairs.append((band * spots + spot, (b2 % bands) * spots + (z2 * YS + y2 % YS) * CORES + c2))
        return lax.ppermute(value, ("band", "grid"), pairs)

    def swap_cores(value):
        return move(value, lambda b, z, y, c: (b, z, y, 1 - c))

    def shift(value, steps):
        return move(value, lambda b, z, y, c: (b + steps, z, y, c))

    def there_and_across(values, steps):
        return [shift(values[0], steps), move(values[1], lambda b, z, y, c: (b + steps, z, y, 1 - c))]

    def along_y(messages, sign):
        return [messages[0]] + [
            move(messages[k], lambda b, z, y, c, k=k: (b, z, y + YS + sign * k, c)) for k in range(1, YS)
        ]

    chips, runs = tables()[5:7]
    blocks = orbitals.reshape(NSUB * SUB, PLANES, GRID, GRID).transpose(0, 2, 1, 3)
    blocks = blocks.reshape(NSUB * SUB, ROWS, GRID)
    both = (blocks, swap_cores(blocks))
    index, *sends, token = pick(plan, both)
    parts = [shift(sends[0], 1), shift(sends[1], -2)]
    own, token = pick_own(token, index, both)
    chains = [{} for _ in CHAINS]

    def start(at):
        nonlocal token
        step, members = CHAINS[at]
        chain = chains[at]
        chain["spec"], sums, token = forward(token, step, members, own, parts[step])
        chain["sums"] = along_y(sums, 1)

    def run(at, after=()):
        nonlocal token
        chain = chains[at]
        (chain["run"],), token = small(run_kernel, token, [*chain["sums"], chips], 1, "run", after=after)
        chain["near"] = move(chain["run"], lambda b, z, y, c: (b, z ^ 1, y, c))

    def two(at):
        nonlocal token
        chain = chains[at]
        (chain["two"],), token = small(two_kernel, token, [chain["run"], chain["near"], runs], 1, "two")
        chain["far"] = move(chain["two"], lambda b, z, y, c: (b, z ^ 2, y, c))

    def edges(at, after=()):
        nonlocal token
        chain = chains[at]
        args = [*chain["sums"], chain["near"], chain["two"], chain["far"], chips, runs]
        outs, token = small(
            edges_kernel, token, args, YS, "edges", [pltpu.VMEM((YS, *chain["run"].shape), F32)], after
        )
        chain["edges"] = along_y(outs, -1)

    def finish(at, prior=(), extra=()):
        nonlocal token
        step, members = CHAINS[at]
        chain = chains[at]
        terms, sums, token = backward(
            token, step, members, chain["spec"], chain["edges"], own, parts[step], prior, extra
        )
        return terms, sums

    second, first, last = range(len(CHAINS))
    start(second)
    run(second)
    start(first)
    two(second)
    start(last)
    run(first)
    run(last)
    edges(second)
    two(first)
    two(last)
    edges(first)
    terms_b, sums_b = finish(second)
    edges(last)
    terms_a, sums_a = finish(first)
    back_a = shift(terms_a, -1)
    terms_a, sums_a = finish(last, sums_a, sums_b[1:])
    back_last = shift(terms_a, -1)
    final = [back_last, swap_cores(back_last[1:])]
    back_b = there_and_across((terms_b[:1], terms_b[1:]), 2)
    total, token = add_early(token, index, [sums_a[0], sums_b[0]])
    total, token = add_middle(
        token, index, [total, swap_cores(sums_a[1]), *back_b, back_a, swap_cores(back_a[1:])]
    )
    total = add_late(token, index, total, final)
    total = total.reshape(NSUB * SUB, GRID, PLANES, GRID).transpose(0, 2, 1, 3)
    return total.reshape(NSUB * SUB, PLANES, GRID * GRID)


def solution(mesh):
    in_specs = (P("band", "grid", None), P())
    out_specs = P("band", "grid", None)
    return jax.shard_map(body, mesh=mesh, in_specs=in_specs, out_specs=out_specs, check_vma=False)
```
